32 devices in a mesh: tok: 8 (over z, x), feat: 4 (over y, core).
Axes of the slice: x: 2, y: 2, z: 4, core: 2. Of those that a mesh axis runs over, the one named last changes fastest.
Arguments:
- tokens: float32 [768, 4096], P('feat', 'tok'), may hold values from -6 to 6
- timesteps: int32 [16], P('tok'), may hold values from 0 to 999
- labels: int32 [16], P('tok'), may hold values from 0 to 1000
- class_table: bfloat16 [768, 1001], P('feat'), may hold values from -6 to 6
- ada_weight: bfloat16 [6, 768, 768], P(None, 'tok', 'feat'), may hold values from -0.21875 to 0.21875
- ada_bias: float32 [6, 768], P(None, 'feat'), may hold values from -3 to 3
- qkv_weight: bfloat16 [3, 768, 768], P(None, 'tok', 'feat'), may hold values from -0.21875 to 0.21875
- qv_bias: float32 [2, 768], P(None, 'feat'), may hold values from -2 to 2
- proj_weight: bfloat16 [768, 768], P('tok', 'feat'), may hold values from -0.875 to 0.875
- proj_bias: float32 [768], P('feat'), may hold values from -2 to 2
- fc1_weight: bfloat16 [768, 3072], P('tok', 'feat'), may hold values from -0.21875 to 0.21875
- fc1_bias: float32 [3072], P('feat'), may hold values from -2 to 2
- fc2_weight: bfloat16 [768, 3072], P('tok', 'feat'), may hold values from -0.109375 to 0.109375
- fc2_bias: float32 [768], P('feat'), may hold values from -2 to 2
- cotangent: float32 [768, 4096], P('feat', 'tok'), may hold values from -6 to 6
Outputs:
- output: float32 [768, 4096], P('feat', 'tok')
- tokens_grad: float32 [768, 4096], P('feat', 'tok')
- class_grad: float32 [768, 1001], P('feat')
- ada_weight_grad: float32 [6, 768, 768], P(None, 'tok', 'feat')
- ada_bias_grad: float32 [6, 768], P(None, 'feat')
- qkv_weight_grad: float32 [3, 768, 768], P(None, 'tok', 'feat')
- qv_bias_grad: float32 [2, 768], P(None, 'feat')
- proj_weight_grad: float32 [768, 768], P('tok', 'feat')
- proj_bias_grad: float32 [768], P('feat')
- fc1_weight_grad: float32 [768, 3072], P('tok', 'feat')
- fc1_bias_grad: float32 [3072], P('feat')
- fc2_weight_grad: float32 [768, 3072], P('tok', 'feat')
- fc2_bias_grad: float32 [768], P('feat')
The draws below stay inside these ranges and needn't reach their ends.
All inputs are finite; a program needn't handle non-finite values.
Results may differ from the reference program's by a relative error of at most 0.02.
The reference program's roundings to bfloat16 on the way count: a program that leaves them out, or rounds other values in their place, can miss the bound.
Values may be sent and summed in bfloat16 or wider, within the bound.
A program may use at most 128 MiB of HBM per device.

```python
import math
import jax
import jax.numpy as jnp
from jax import lax

D = 768
HEADS = 12
HEAD_DIM = 64
FF = 3072
CLASSES = 1001
SEQ = 256
LATENTS = 16
TOKENS = 4096


def set_ends(drawn, key, smallest, high):
    longest = drawn.shape.index(max(drawn.shape))
    spots = []
    for shift in (0, 1):
        where = [jax.random.randint(jax.random.fold_in(key, axis), (), 0, length) for axis, length in enumerate(drawn.shape)]
        where[longest] = (where[longest] + shift) % drawn.shape[longest]
        spots.append(tuple(where))
    return drawn.at[spots[0]].set(smallest).at[spots[1]].set(high)


def levels(rng, shape, cuts, low, high):
    gain = 1.0
    for axis_at, parts in cuts:
        steps = jax.random.uniform(jax.random.fold_in(jax.random.fold_in(rng, 6), axis_at), (parts,), jnp.float32, low / len(cuts), high / len(cuts))
        gain = gain * jnp.repeat(jnp.exp(steps), shape[axis_at] // parts).reshape((-1,) + (1,) * (len(shape) - 1 - axis_at))
    return gain


def gaussian(own_key, dims, width, reach, shards=(), kind=jnp.bfloat16):
    drawn = width * jax.random.normal(own_key, dims, jnp.float32)
    if shards:
        drawn = drawn * levels(own_key, dims, shards, -0.22, 0.18)
    return jnp.clip(drawn, -reach, reach).astype(kind)


def setup_inputs(seed: int = 0) -> dict:
    key_of = jax.random.split(jax.random.key(seed), 16)
    tokens = gaussian(key_of[0], (D, TOKENS), 1.0, 6.0, ((0, 4), (1, 8)), jnp.float32)
    timesteps = set_ends(jax.random.randint(key_of[1], (LATENTS,), 0, 1000), jax.random.fold_in(key_of[1], 1), 0, 999).astype(jnp.int32)
    labels = set_ends(jax.random.randint(key_of[2], (LATENTS,), 0, CLASSES), jax.random.fold_in(key_of[2], 1), 0, CLASSES - 1).astype(jnp.int32)
    class_table = gaussian(key_of[3], (D, CLASSES), 1.0, 6.0, ((0, 4),))
    ada_weight = gaussian(key_of[4], (6, D, D), D ** -0.5, 0.21875, ((1, 8), (2, 4)))
    ada_bias = gaussian(key_of[5], (6, D), 0.5, 3.0, ((1, 4),), jnp.float32)
    qkv_weight = gaussian(key_of[6], (3, D, D), D ** -0.5, 0.21875, ((1, 8), (2, 4)))
    qv_bias = gaussian(key_of[7], (2, D), 0.3, 2.0, ((1, 4),), jnp.float32)
    proj_weight = gaussian(key_of[8], (D, D), (D // 16) ** -0.5, 0.875, ((0, 8), (1, 4)))
    proj_bias = gaussian(key_of[9], (D,), 0.3, 2.0, ((0, 4),), jnp.float32)
    fc1_weight = gaussian(key_of[10], (D, FF), D ** -0.5, 0.21875, ((0, 8), (1, 4)))
    fc1_bias = gaussian(key_of[11], (FF,), 0.3, 2.0, ((0, 4),), jnp.float32)
    fc2_weight = gaussian(key_of[12], (D, FF), FF ** -0.5, 0.109375, ((0, 8), (1, 4)))
    fc2_bias = gaussian(key_of[13], (D,), 0.3, 2.0, ((0, 4),), jnp.float32)
    cotangent = gaussian(key_of[14], (D, TOKENS), 1.0, 6.0, ((0, 4), (1, 8)), jnp.float32)
    return dict(tokens=tokens, timesteps=timesteps, labels=labels, class_table=class_table, ada_weight=ada_weight, ada_bias=ada_bias, qkv_weight=qkv_weight, qv_bias=qv_bias, proj_weight=proj_weight, proj_bias=proj_bias, fc1_weight=fc1_weight, fc1_bias=fc1_bias, fc2_weight=fc2_weight, fc2_bias=fc2_bias, cotangent=cotangent)


@jax.custom_vjp
def low(v):
    return lax.optimization_barrier(v.astype(jnp.bfloat16)).astype(jnp.float32)

@jax.custom_vjp
def low_back(v):
    return v

def low_keep(v):
    return (low(v), None)

def low_pass(kept, grad):
    return (grad,)

def back_keep(v):
    return (v, None)

def back_low(kept, grad):
    return (low(grad),)
low.defvjp(low_keep, low_pass)
low_back.defvjp(back_keep, back_low)

def product(form, left, right):
    return jnp.einsum(form, left, right, precision=lax.Precision.HIGHEST)

def time_features(step_ids, feat_count):
    half_width = feat_count // 2
    frequency = jnp.exp(-math.log(10000.0) * jnp.arange(half_width, dtype=jnp.float32) / half_width)
    angles = step_ids.astype(jnp.float32)[:, None] * frequency[None, :]
    return jnp.concatenate([jnp.cos(angles), jnp.sin(angles)], axis=-1)

def norm_rows(values_in):
    mean_val = lax.optimization_barrier(jnp.mean(values_in, -1, keepdims=True))
    centered = values_in - mean_val
    variance = lax.optimization_barrier(jnp.mean(centered * centered, -1, keepdims=True))
    return centered * lax.rsqrt(variance + 1e-06)

def block_forward(field_in, condition, ada_weight, ada_bias, qkv_weight, qv_bias, proj_weight, proj_bias, fc1_weight, fc1_bias, fc2_weight, fc2_bias):
    group_size = condition.shape[0]
    cond_act = low(jax.nn.silu(condition))
    modulation = low_back(product('lk,jkc->ljc', cond_act, ada_weight) + ada_bias[None])
    modulation = modulation[:, :, None, :]
    field_three = field_in.reshape(group_size, SEQ, D)
    hidden_one = low(norm_rows(field_three) * (1.0 + modulation[:, 1]) + modulation[:, 0]).reshape(-1, D)
    projected = product('rk,jkc->jrc', hidden_one, qkv_weight)
    queries = low(low_back(projected[0] + qv_bias[0]))
    keys_all = low(low_back(projected[1]))
    values_all = low(low_back(projected[2] + qv_bias[1]))
    head_shape = (group_size, SEQ, HEADS, HEAD_DIM)
    scores = low_back(product('lqhd,lkhd->lhqk', queries.reshape(head_shape), keys_all.reshape(head_shape)) * HEAD_DIM ** (-0.5))
    probs = low(jax.nn.softmax(scores, axis=-1))
    attended = low(low_back(product('lhqk,lkhd->lqhd', probs, values_all.reshape(head_shape)))).reshape(-1, D)
    attn_out = low_back(product('rc,oc->ro', attended, proj_weight) + proj_bias).reshape(group_size, SEQ, D)
    middle = field_three + modulation[:, 2] * attn_out
    hidden_two = low(norm_rows(middle) * (1.0 + modulation[:, 4]) + modulation[:, 3]).reshape(-1, D)
    pre_act = low_back(product('rk,kf->rf', hidden_two, fc1_weight) + fc1_bias)
    act_low = low(jax.nn.gelu(pre_act, approximate=True))
    mlp_out = low_back(product('rf,of->ro', act_low, fc2_weight) + fc2_bias).reshape(group_size, SEQ, D)
    return (middle + modulation[:, 5] * mlp_out).reshape(-1, D)

def reference(tokens, timesteps, labels, class_table, ada_weight, ada_bias, qkv_weight, qv_bias, proj_weight, proj_bias, fc1_weight, fc1_bias, fc2_weight, fc2_bias, cotangent):
    params = (class_table.astype(jnp.float32).T, ada_weight.astype(jnp.float32), ada_bias.astype(jnp.float32), qkv_weight.astype(jnp.float32), qv_bias.astype(jnp.float32), proj_weight.astype(jnp.float32), proj_bias.astype(jnp.float32), fc1_weight.astype(jnp.float32), fc1_bias.astype(jnp.float32), fc2_weight.astype(jnp.float32), fc2_bias.astype(jnp.float32))
    group_size = math.gcd(LATENTS, 16)
    group_count = LATENTS // group_size
    field_groups = tokens.T.reshape(group_count, group_size * SEQ, D)
    cot_groups = cotangent.T.reshape(group_count, group_size * SEQ, D)
    step_groups = timesteps.reshape(group_count, group_size)
    label_groups = labels.reshape(group_count, group_size)

    def one_group(grad_totals, inputs):
        field_in, step_ids, label_ids, cot_in = inputs

        def run(values_in, weights):
            table = weights[0]
            condition = table[label_ids] + time_features(step_ids, D)
            return block_forward(values_in, condition, *weights[1:])
        result, pullback = jax.vjp(run, field_in, params)
        grad_field, grad_params = pullback(cot_in)
        grad_totals = jax.tree.map(jnp.add, grad_totals, grad_params)
        return (grad_totals, (result, grad_field))
    zeros_init = jax.tree.map(jnp.zeros_like, params)
    grad_totals, (results, grad_fields) = lax.scan(one_group, zeros_init, (field_groups, step_groups, label_groups, cot_groups))
    return (results.reshape(TOKENS, D).T, grad_fields.reshape(TOKENS, D).T, grad_totals[0].T, grad_totals[1], grad_totals[2], grad_totals[3], grad_totals[4], grad_totals[5], grad_totals[6], grad_totals[7], grad_totals[8], grad_totals[9], grad_totals[10])
```

```python
from functools import partial
import math

import jax
import jax.numpy as jnp
from jax import lax
from jax.experimental import pallas as pl
from jax.experimental.pallas import tpu as pltpu
from jax.sharding import PartitionSpec as P

D = 768
HEAD_DIM = 64
FEAT = 4
MESH = pl.DeviceIdType.MESH
F32 = jnp.float32
BF16 = jnp.bfloat16
VMEM = pl.BlockSpec(memory_space=pltpu.VMEM)


def time_features(step_ids, feat_count):
    half_width = feat_count // 2
    frequency = jnp.exp(-math.log(10000.0) * jnp.arange(half_width, dtype=jnp.float32) / half_width)
    angles = step_ids.astype(jnp.float32)[:, None] * frequency[None, :]
    return jnp.concatenate([jnp.cos(angles), jnp.sin(angles)], axis=-1)


def partners():
    f = lax.axis_index("feat")
    near = f + 1 - 2 * (f % 2)
    far = (f + 2) % FEAT
    return f, near, far, (near + 2) % FEAT


def greet(near, far, cross):
    barrier = pltpu.get_barrier_semaphore()
    for peer in (near, far, cross):
        pl.semaphore_signal(barrier, inc=1, device_id={"feat": peer}, device_id_type=MESH)
    pl.semaphore_wait(barrier, 3)


def push(src, dst, sems, at, peer):
    return pltpu.make_async_remote_copy(
        src_ref=src,
        dst_ref=dst,
        send_sem=sems.at[0, at],
        recv_sem=sems.at[1, at],
        device_id={"feat": peer},
        device_id_type=MESH,
    )


def gather_start(buf, sems, base):
    f, near, far, _ = partners()
    to_far = push(buf.at[f], buf.at[f], sems, base, far)
    to_near = push(buf.at[f], buf.at[f], sems, base + 1, near)
    to_far.start()
    to_near.start()
    return to_far, to_near


def gather_forward(buf, sems, base, started):
    _, near, far, _ = partners()
    started[0].wait_recv()
    relay = push(buf.at[far], buf.at[far], sems, base + 2, near)
    relay.start()
    return relay


def gather_finish(buf, out, started, relay):
    started[1].wait_recv()
    relay.wait_recv()
    for copy in (*started, relay):
        copy.wait_send()
    width = buf.shape[2]
    for block in range(FEAT):
        out[:, block * width : (block + 1) * width] = buf[block]


def scatter_start(term, buf, near_in, sems, base):
    f, near, _, _ = partners()
    side, core = f // 2, f % 2
    width = buf.shape[2]
    for block in range(FEAT):
        buf[block] = term[:, block * width : (block + 1) * width]
    first = push(buf.at[2 * (1 - side) + 1 - core], near_in.at[0], sems, base, near)
    second = push(buf.at[2 * side + 1 - core], near_in.at[1], sems, base + 1, near)
    first.start()
    second.start()
    return first, second


def scatter_cross(buf, near_in, out_buf, far_in, sems, base, started):
    _, _, far, _ = partners()
    started[0].wait_recv()
    out_buf[...] = (buf[far].astype(F32) + near_in[0].astype(F32)).astype(BF16)
    cross = push(out_buf, far_in, sems, base + 2, far)
    cross.start()
    return cross


def scatter_finish(buf, near_in, far_in, started, cross):
    f, _, _, _ = partners()
    started[1].wait_recv()
    own = buf[f].astype(F32) + near_in[1].astype(F32)
    cross.wait_recv()
    for copy in (*started, cross):
        copy.wait_send()
    return own + far_in[...].astype(F32)


def swap_rows(pair, stats, sems, base):
    _, near, far, cross = partners()
    rows = pair[0].shape[0]
    lane = lax.broadcasted_iota(jnp.int32, (rows, 128), 1)
    packed = jnp.where(lane == 0, pair[0], jnp.where(lane == 1, pair[1], 0.0))
    stats[0] = packed.T[:8]
    copies = [
        push(stats.at[0], stats.at[slot], sems, base + slot - 1, peer)
        for slot, peer in ((1, near), (2, far), (3, cross))
    ]
    for copy in copies:
        copy.start()
    for copy in copies:
        copy.wait()
    return stats[...]


def columns(first, second):
    rows = first.shape[1]
    tall = jnp.concatenate([first, second, jnp.zeros((126, rows), F32)], 0).T
    return tall[:, 0:1], tall[:, 1:2]


def norm_stats(values, stats, sems, base):
    width = values.shape[1]
    local = jnp.sum(values, 1, keepdims=True)
    off = values - local / width
    got = swap_rows((local, jnp.sum(off * off, 1, keepdims=True)), stats, sems, base)
    sums, squares = got[:, 0], got[:, 1]
    mean = jnp.sum(sums, 0, keepdims=True) / D
    shifted = sums / width - mean
    variance = jnp.sum(squares + width * shifted * shifted, 0, keepdims=True) / D
    return columns(mean, lax.rsqrt(variance + 1e-06))


def norm_grad(grad_norm, normed, inverse, stats, sems, base):
    got = swap_rows(
        (jnp.sum(grad_norm, 1, keepdims=True), jnp.sum(grad_norm * normed, 1, keepdims=True)),
        stats,
        sems,
        base,
    )
    total = jnp.sum(got, 0)
    first, second = columns(total[0:1] / D, total[1:2] / D)
    return inverse * (grad_norm - first - normed * second)


def spread(mod, which, rows):
    count = mod.shape[0] // 6
    return jnp.concatenate(
        [
            jnp.broadcast_to(mod[l * 6 + which : l * 6 + which + 1], (rows // count, mod.shape[1]))
            for l in range(count)
        ],
        0,
    )


def latent_sums(out, values, which, kinds):
    count = out.shape[0] // kinds
    seq = values.shape[0] // count
    for l in range(count):
        row = l * kinds + which
        out[row : row + 1] = jnp.sum(values[l * seq : (l + 1) * seq], 0, keepdims=True)


def open_kernel(x, mod, grad_out, full, grad_full, normed_out, inverse_out, fc2_sum, buf, grad_buf, stats, sems):
    f, near, far, cross = partners()
    rows = x.shape[0]
    mods = mod[...]
    greet(near, far, cross)
    grad_mlp = (grad_out[...] * spread(mods, 5, rows)).astype(BF16)
    fc2_sum[...] = jnp.sum(grad_mlp.astype(F32), 0, keepdims=True)
    grad_buf[f] = grad_mlp
    values = x[...]
    mean, inverse = norm_stats(values, stats, sems, 0)
    normed = (values - mean) * inverse
    normed_out[...] = normed
    inverse_out[...] = inverse
    buf[f] = (normed * (1.0 + spread(mods, 1, rows)) + spread(mods, 0, rows)).astype(BF16)
    started = gather_start(buf, sems, 3)
    grad_started = gather_start(grad_buf, sems, 6)
    relay = gather_forward(buf, sems, 3, started)
    gather_finish(buf, full, started, relay)
    grad_relay = gather_forward(grad_buf, sems, 6, grad_started)
    gather_finish(grad_buf, grad_full, grad_started, grad_relay)


def middle_kernel(
    term, x, mod, bias, attn_out, middle_out, normed_out, inverse_out, full,
    sbuf, near_in, out_buf, far_in, buf, stats, sems,
):
    f, near, far, cross = partners()
    rows = x.shape[0]
    mods = mod[...]
    greet(near, far, cross)
    started = scatter_start(term, sbuf, near_in, sems, 0)
    crossing = scatter_cross(sbuf, near_in, out_buf, far_in, sems, 0, started)
    attn = scatter_finish(sbuf, near_in, far_in, started, crossing) + bias[...]
    attn_out[...] = attn
    middle = x[...] + spread(mods, 2, rows) * attn
    middle_out[...] = middle
    mean, inverse = norm_stats(middle, stats, sems, 3)
    normed = (middle - mean) * inverse
    normed_out[...] = normed
    inverse_out[...] = inverse
    buf[f] = (normed * (1.0 + spread(mods, 4, rows)) + spread(mods, 3, rows)).astype(BF16)
    gathering = gather_start(buf, sems, 6)
    relay = gather_forward(buf, sems, 6, gathering)
    gather_finish(buf, full, gathering, relay)


def back_kernel(
    term, mlp_term, grad_out, normed_in, inverse_in, mod, bias, middle, attn,
    grad_middle_out, full, output, sums, proj_sum,
    sbuf, near_in, out_buf, far_in, mbuf, mnear, mout, mfar, buf, stats, sems,
):
    f, near, far, cross = partners()
    rows = grad_out.shape[0]
    mods = mod[...]
    greet(near, far, cross)
    started = scatter_start(term, sbuf, near_in, sems, 0)
    mlp_started = scatter_start(mlp_term, mbuf, mnear, sems, 3)
    crossing = scatter_cross(sbuf, near_in, out_buf, far_in, sems, 0, started)
    grad_hidden = scatter_finish(sbuf, near_in, far_in, started, crossing)
    normed = normed_in[...]
    grad_middle = grad_out[...] + norm_grad(
        grad_hidden * (1.0 + spread(mods, 4, rows)), normed, inverse_in[...], stats, sems, 6
    )
    grad_attn = (grad_middle * spread(mods, 2, rows)).astype(BF16)
    buf[f] = grad_attn
    gathering = gather_start(buf, sems, 9)
    mlp_crossing = scatter_cross(mbuf, mnear, mout, mfar, sems, 3, mlp_started)
    grad_middle_out[...] = grad_middle
    proj_sum[...] = jnp.sum(grad_attn.astype(F32), 0, keepdims=True)
    latent_sums(sums, grad_hidden, 0, 4)
    latent_sums(sums, grad_hidden * normed, 1, 4)
    latent_sums(sums, grad_middle * attn[...], 2, 4)
    relay = gather_forward(buf, sems, 9, gathering)
    gather_finish(buf, full, gathering, relay)
    mlp_out = scatter_finish(mbuf, mnear, mfar, mlp_started, mlp_crossing) + bias[...]
    output[...] = middle[...] + spread(mods, 5, rows) * mlp_out
    latent_sums(sums, grad_out[...] * mlp_out, 3, 4)


def close_kernel(
    term, normed_in, inverse_in, mod, grad_middle, tokens_grad, sums,
    sbuf, near_in, out_buf, far_in, stats, sems,
):
    _, near, far, cross = partners()
    rows = normed_in.shape[0]
    mods = mod[...]
    greet(near, far, cross)
    started = scatter_start(term, sbuf, near_in, sems, 0)
    crossing = scatter_cross(sbuf, near_in, out_buf, far_in, sems, 0, started)
    grad_hidden = scatter_finish(sbuf, near_in, far_in, started, crossing)
    normed = normed_in[...]
    tokens_grad[...] = grad_middle[...] + norm_grad(
        grad_hidden * (1.0 + spread(mods, 1, rows)), normed, inverse_in[...], stats, sems, 3
    )
    latent_sums(sums, grad_hidden, 0, 2)
    latent_sums(sums, grad_hidden * normed, 1, 2)


def mod_kernel(count, term, bias, out, recv, sems):
    t = lax.axis_index("tok")
    barrier = pltpu.get_barrier_semaphore()
    for step in range(1, count):
        pl.semaphore_signal(
            barrier, inc=1, device_id={"tok": (t + step) % count}, device_id_type=MESH
        )
    pl.semaphore_wait(barrier, count - 1)
    copies = []
    for step in range(1, count):
        peer = (t + step) % count
        copies.append(
            pltpu.make_async_remote_copy(
                src_ref=term.at[peer],
                dst_ref=recv.at[step - 1],
                send_sem=sems.at[0, step - 1],
                recv_sem=sems.at[1, step - 1],
                device_id={"tok": peer},
                device_id_type=MESH,
            )
        )
    for copy in copies:
        copy.start()
    for copy in copies:
        copy.wait()
    out[...] = term[t] + jnp.sum(recv[...], 0) + bias[...]


def call(kernel, collective_id, outs, scratch, sem_count, *args):
    out_shape = [jax.ShapeDtypeStruct(shape, dtype) for shape, dtype in outs]
    return pl.pallas_call(
        kernel,
        out_shape=out_shape,
        in_specs=[VMEM] * len(args),
        out_specs=[VMEM] * len(outs),
        scratch_shapes=[pltpu.VMEM(shape, dtype) for shape, dtype in scratch]
        + [pltpu.SemaphoreType.DMA((2, sem_count))],
        compiler_params=pltpu.CompilerParams(
            collective_id=collective_id, has_side_effects=True, vmem_limit_bytes=40 * 2**20
        ),
    )(*args)


def bits_of(count):
    return [count >> (i + 1) for i in range(count.bit_length() - 1)]


def pick(values, axis, at):
    return jnp.where(
        at == 0, lax.index_in_dim(values, 0, axis, False), lax.index_in_dim(values, 1, axis, False)
    )


def gather_rows(block, row_axis, count, order):
    t = lax.axis_index("tok")
    bits = bits_of(count)
    seen = []
    held = block
    for bit in [bits[i] for i in order]:
        other = lax.ppermute(held, "tok", [(i, i ^ bit) for i in range(count)])
        axis = row_axis + sum(1 for b in seen if b > bit)
        low = (t // bit) % 2 == 0
        held = jnp.stack(
            [jnp.where(low, held, other), jnp.where(low, other, held)], axis
        )
        seen.append(bit)
    shape = list(block.shape)
    shape[row_axis] *= count
    return held.reshape(shape)


def scatter_rows(grad, row_axis, count, order):
    t = lax.axis_index("tok")
    bits = bits_of(count)
    shape = list(grad.shape)
    rows = shape[row_axis] // count
    held = grad.reshape(shape[:row_axis] + [2] * len(bits) + [rows] + shape[row_axis + 1 :])
    left = list(bits)
    for bit in [bits[i] for i in order]:
        axis = row_axis + left.index(bit)
        mine = (t // bit) % 2
        sent = pick(held, axis, 1 - mine).astype(BF16)
        got = lax.ppermute(sent, "tok", [(i, i ^ bit) for i in range(count)])
        held = pick(held, axis, mine).astype(F32) + got.astype(F32)
        left.remove(bit)
    return held


def per_device(
    tok_count,
    tokens,
    timesteps,
    labels,
    class_table,
    ada_weight,
    ada_bias,
    qkv_weight,
    qv_bias,
    proj_weight,
    proj_bias,
    fc1_weight,
    fc1_bias,
    fc2_weight,
    fc2_bias,
    cotangent,
):
    width, rows = tokens.shape
    lat = timesteps.shape[0]
    seq_len = rows // lat
    head_count = width // HEAD_DIM
    score_scale = HEAD_DIM ** (-0.5)
    feat_at, tok_at = lax.axis_index("feat"), lax.axis_index("tok")
    offset = feat_at * width
    head_shape = (lat, seq_len, head_count, HEAD_DIM)
    part = ada_weight.shape[1]
    levels = len(bits_of(tok_count))
    down = list(range(levels))
    mixed = [levels - 1] + list(range(levels - 1))

    waves = lax.dynamic_slice_in_dim(time_features(timesteps, D), offset, width, 1)
    condition = jnp.take(class_table, labels, axis=1).T.astype(F32) + waves
    cond_all = lax.all_gather(condition, ("tok", "feat"), axis=0, tiled=False)
    cond_all = (
        cond_all.reshape(tok_count, FEAT, lat, width)
        .transpose(0, 2, 1, 3)
        .reshape(tok_count * lat, D)
    )
    labels_all = lax.all_gather(labels, "tok", axis=0, tiled=True)
    qkv_full = gather_rows(qkv_weight, 1, tok_count, down)
    proj_full = gather_rows(proj_weight, 0, tok_count, mixed)
    fc1_full = gather_rows(fc1_weight, 0, tok_count, mixed)
    fc2_full = gather_rows(fc2_weight, 0, tok_count, down)

    cond_rows = jax.nn.silu(
        lax.dynamic_slice_in_dim(cond_all, tok_at * part, part, 1)
    ).astype(BF16)
    mod_term = jnp.einsum("lk,jkc->ljc", cond_rows, ada_weight, preferred_element_type=F32)
    mod_term = mod_term.reshape(tok_count, lat * 6, width)
    (mod,) = call(
        partial(mod_kernel, tok_count),
        0,
        [((lat * 6, width), F32)],
        [((tok_count - 1, lat * 6, width), F32)],
        tok_count - 1,
        mod_term,
        jnp.tile(ada_bias, (lat, 1)),
    )

    own_f32 = ((rows, width), F32)
    own_low = ((rows, width), BF16)
    one_f32 = ((rows, 1), F32)
    full_low = ((rows, D), BF16)
    line = ((1, width), F32)
    buf = ((FEAT, rows, width), BF16)
    stats = ((FEAT, 8, rows), F32)
    scatter_bufs = [buf, ((2, rows, width), BF16), own_low, own_low]

    field_in = tokens.T
    grad_out = cotangent.T
    full_one, grad_mlp_full, normed_one, inverse_one, fc2_bias_grad = call(
        open_kernel,
        1,
        [full_low, full_low, own_f32, one_f32, line],
        [buf, buf, stats],
        9,
        field_in,
        mod,
        grad_out,
    )
    projected = jnp.einsum("rk,jkc->jrc", full_one, qkv_full, preferred_element_type=F32)
    queries = (projected[0] + qv_bias[0]).astype(BF16).reshape(head_shape)
    keys_low = projected[1].astype(BF16).reshape(head_shape)
    values_low = (projected[2] + qv_bias[1]).astype(BF16).reshape(head_shape)
    scores = (
        jnp.einsum("lqhd,lkhd->lhqk", queries, keys_low, preferred_element_type=F32) * score_scale
    )
    top_score = jnp.max(scores, -1, keepdims=True)
    exponent = jnp.exp(scores - top_score)
    exp_sums = jnp.sum(exponent, -1, keepdims=True)
    probs = exponent / exp_sums
    probs_low = probs.astype(BF16)
    attended = jnp.einsum("lhqk,lkhd->lqhd", probs_low, values_low, preferred_element_type=F32)
    attended = attended.astype(BF16).reshape(rows, width)
    attn_term = jnp.einsum("rc,oc->ro", attended, proj_full, preferred_element_type=F32)
    attn_out, middle, normed_two, inverse_two, full_two = call(
        middle_kernel,
        2,
        [own_f32, own_f32, own_f32, one_f32, full_low],
        scatter_bufs + [buf, stats],
        9,
        attn_term.astype(BF16),
        field_in,
        mod,
        proj_bias[None],
    )
    pre_act = jnp.dot(full_two, fc1_full, preferred_element_type=F32) + fc1_bias
    act_value, gelu_back = jax.vjp(partial(jax.nn.gelu, approximate=True), pre_act)
    act_low = act_value.astype(BF16)
    grad_act = jnp.dot(grad_mlp_full, fc2_full, preferred_element_type=F32)
    grad_pre = gelu_back(grad_act)[0].astype(BF16)
    mlp_term = jnp.einsum("rf,of->ro", act_low, fc2_full, preferred_element_type=F32)
    hidden_two_term = jnp.einsum("rf,kf->rk", grad_pre, fc1_full, preferred_element_type=F32)
    grad_middle, grad_attn_full, output, two_sums, proj_bias_grad = call(
        back_kernel,
        3,
        [own_f32, full_low, own_f32, ((lat * 4, width), F32), line],
        scatter_bufs + scatter_bufs + [buf, stats],
        12,
        hidden_two_term.astype(BF16),
        mlp_term.astype(BF16),
        grad_out,
        normed_two,
        inverse_two,
        mod,
        fc2_bias[None],
        middle,
        attn_out,
    )
    fc2_grad = jnp.einsum("ro,rf->of", grad_mlp_full, act_low, preferred_element_type=F32)
    fc2_shard = scatter_rows(fc2_grad.astype(BF16), 0, tok_count, down[::-1])
    fc1_bias_grad = jnp.sum(grad_pre, 0, dtype=F32)
    fc1_grad = jnp.einsum("rk,rf->kf", full_two, grad_pre, preferred_element_type=F32)
    fc1_shard = scatter_rows(fc1_grad.astype(BF16), 0, tok_count, mixed[::-1])
    proj_grad = jnp.einsum("ro,rc->oc", grad_attn_full, attended, preferred_element_type=F32)
    proj_shard = scatter_rows(proj_grad.astype(BF16), 0, tok_count, mixed[::-1])
    grad_attended = (
        jnp.dot(grad_attn_full, proj_full, preferred_element_type=F32)
        .astype(BF16)
        .reshape(head_shape)
    )
    grad_values = jnp.einsum(
        "lhqk,lqhd->lkhd", probs_low, grad_attended, preferred_element_type=F32
    )
    grad_probs = jnp.einsum(
        "lqhd,lkhd->lhqk", grad_attended, values_low, preferred_element_type=F32
    )
    grad_scores = (
        probs * (grad_probs - jnp.sum(grad_probs * probs, -1, keepdims=True))
    ).astype(BF16)
    grad_queries = (
        jnp.einsum("lhqk,lkhd->lqhd", grad_scores, keys_low, preferred_element_type=F32)
        * score_scale
    )
    grad_keys = (
        jnp.einsum("lhqk,lqhd->lkhd", grad_scores, queries, preferred_element_type=F32)
        * score_scale
    )
    grad_qkv = (
        jnp.stack([grad_queries, grad_keys, grad_values]).astype(BF16).reshape(3, rows, width)
    )
    hidden_one_term = jnp.einsum("jrc,jkc->rk", grad_qkv, qkv_full, preferred_element_type=F32)
    tokens_grad, one_sums = call(
        close_kernel,
        4,
        [own_f32, ((lat * 2, width), F32)],
        scatter_bufs + [stats],
        6,
        hidden_one_term.astype(BF16),
        normed_one,
        inverse_one,
        mod,
        grad_middle,
    )
    qkv_grad = jnp.einsum("rk,jrc->jkc", full_one, grad_qkv, preferred_element_type=F32)
    qkv_shard = scatter_rows(qkv_grad.astype(BF16), 1, tok_count, down[::-1])
    qv_bias_grad = jnp.stack([jnp.sum(grad_qkv[0], 0, dtype=F32), jnp.sum(grad_qkv[2], 0, dtype=F32)])

    ones = one_sums.reshape(lat, 2, width)
    twos = two_sums.reshape(lat, 4, width)
    grad_mod = jnp.stack(
        [ones[:, 0], ones[:, 1], twos[:, 2], twos[:, 0], twos[:, 1], twos[:, 3]], 1
    ).astype(BF16)
    bias_terms = jnp.concatenate(
        [qv_bias_grad.reshape(-1), proj_bias_grad[0], fc1_bias_grad, fc2_bias_grad[0]]
    )
    bias_sums = lax.psum(bias_terms, "tok")
    grad_mod_all = lax.all_gather(grad_mod, "tok", axis=0, tiled=True)
    ada_bias_sum = jnp.sum(grad_mod_all, 0, dtype=F32)
    ada_shard = jnp.einsum("lk,ljc->jkc", cond_rows, grad_mod_all, preferred_element_type=F32)
    cond_term = jnp.einsum("ljc,jkc->lk", grad_mod_all, ada_weight, preferred_element_type=F32)
    cond_terms = lax.all_gather(cond_term, ("tok", "feat"), axis=0, tiled=False)
    grad_cond_act = (
        jnp.sum(cond_terms.reshape(tok_count, FEAT, tok_count * lat, part), 1)
        .transpose(1, 0, 2)
        .reshape(tok_count * lat, D)
    )
    own_cond = lax.dynamic_slice_in_dim(cond_all, offset, width, 1)
    own_grad = lax.dynamic_slice_in_dim(grad_cond_act, offset, width, 1)
    grad_condition = jax.vjp(jax.nn.silu, own_cond)[1](own_grad)[0]
    class_count = class_table.shape[1]
    one_hot = (
        labels_all[:, None] == jnp.arange(class_count, dtype=jnp.int32)[None, :]
    ).astype(F32)
    class_sum = jnp.einsum("lc,lw->wc", one_hot, grad_condition, precision=lax.Precision.HIGHEST)
    inner = fc1_bias.shape[0]
    return (
        output.T,
        tokens_grad.T,
        class_sum,
        ada_shard,
        ada_bias_sum,
        qkv_shard,
        bias_sums[: 2 * width].reshape(2, width),
        proj_shard,
        bias_sums[2 * width : 3 * width],
        fc1_shard,
        bias_sums[3 * width : 3 * width + inner],
        fc2_shard,
        bias_sums[3 * width + inner :],
    )


def solution(mesh):
    return jax.shard_map(
        partial(per_device, mesh.shape["tok"]),
        mesh=mesh,
        in_specs=(
            P("feat", "tok"),
            P("tok"),
            P("tok"),
            P("feat", None),
            P(None, "tok", "feat"),
            P(None, "feat"),
            P(None, "tok", "feat"),
            P(None, "feat"),
            P("tok", "feat"),
            P("feat"),
            P("tok", "feat"),
            P("feat"),
            P("tok", "feat"),
            P("feat"),
            P("feat", "tok"),
        ),
        out_specs=(
            P("feat", "tok"),
            P("feat", "tok"),
            P("feat", None),
            P(None, "tok", "feat"),
            P(None, "feat"),
            P(None, "tok", "feat"),
            P(None, "feat"),
            P("tok", "feat"),
            P("feat"),
            P("tok", "feat"),
            P("feat"),
            P("tok", "feat"),
            P("feat"),
        ),
        check_vma=False,
    )
```

```python
from functools import partial
import math

import jax
import jax.numpy as jnp
from jax import lax
from jax.experimental import pallas as pl
from jax.experimental.pallas import tpu as pltpu
from jax.sharding import PartitionSpec as P

D = 768
HEAD_DIM = 64
FEAT = 4
MESH = pl.DeviceIdType.MESH
F32 = jnp.float32
BF16 = jnp.bfloat16
VMEM = pl.BlockSpec(memory_space=pltpu.VMEM)


def time_features(step_ids, feat_count):
    half_width = feat_count // 2
    frequency = jnp.exp(-math.log(10000.0) * jnp.arange(half_width, dtype=jnp.float32) / half_width)
    angles = step_ids.astype(jnp.float32)[:, None] * frequency[None, :]
    return jnp.concatenate([jnp.cos(angles), jnp.sin(angles)], axis=-1)


def partners():
    f = lax.axis_index("feat")
    near = f + 1 - 2 * (f % 2)
    far = (f + 2) % FEAT
    return f, near, far, (near + 2) % FEAT


def greet(near, far, cross):
    barrier = pltpu.get_barrier_semaphore()
    for peer in (near, far, cross):
        pl.semaphore_signal(barrier, inc=1, device_id={"feat": peer}, device_id_type=MESH)
    pl.semaphore_wait(barrier, 3)


def push(src, dst, sems, at, peer):
    return pltpu.make_async_remote_copy(
        src_ref=src,
        dst_ref=dst,
        send_sem=sems.at[0, at],
        recv_sem=sems.at[1, at],
        device_id={"feat": peer},
        device_id_type=MESH,
    )


def gather_start(buf, sems, base):
    f, near, far, _ = partners()
    to_far = push(buf.at[f], buf.at[f], sems, base, far)
    to_near = push(buf.at[f], buf.at[f], sems, base + 1, near)
    to_far.start()
    to_near.start()
    return to_far, to_near


def gather_forward(buf, sems, base, started):
    _, near, far, _ = partners()
    started[0].wait_recv()
    relay = push(buf.at[far], buf.at[far], sems, base + 2, near)
    relay.start()
    return relay


def gather_finish(buf, out, started, relay):
    started[1].wait_recv()
    relay.wait_recv()
    for copy in (*started, relay):
        copy.wait_send()
    width = buf.shape[2]
    for block in range(FEAT):
        out[:, block * width : (block + 1) * width] = buf[block]


def scatter_start(term, buf, near_in, sems, base):
    f, near, _, _ = partners()
    side, core = f // 2, f % 2
    width = buf.shape[2]
    for block in range(FEAT):
        buf[block] = term[:, block * width : (block + 1) * width]
    first = push(buf.at[2 * (1 - side) + 1 - core], near_in.at[0], sems, base, near)
    second = push(buf.at[2 * side + 1 - core], near_in.at[1], sems, base + 1, near)
    first.start()
    second.start()
    return first, second


def scatter_cross(buf, near_in, out_buf, far_in, sems, base, started):
    _, _, far, _ = partners()
    started[0].wait_recv()
    out_buf[...] = (buf[far].astype(F32) + near_in[0].astype(F32)).astype(BF16)
    cross = push(out_buf, far_in, sems, base + 2, far)
    cross.start()
    return cross


def scatter_finish(buf, near_in, far_in, started, cross):
    f, _, _, _ = partners()
    started[1].wait_recv()
    own = buf[f].astype(F32) + near_in[1].astype(F32)
    cross.wait_recv()
    for copy in (*started, cross):
        copy.wait_send()
    return own + far_in[...].astype(F32)


def swap_rows(pair, stats, sems, base):
    _, near, far, cross = partners()
    rows = pair[0].shape[0]
    lane = lax.broadcasted_iota(jnp.int32, (rows, 128), 1)
    packed = jnp.where(lane == 0, pair[0], jnp.where(lane == 1, pair[1], 0.0))
    stats[0] = packed.T[:8]
    copies = [
        push(stats.at[0], stats.at[slot], sems, base + slot - 1, peer)
        for slot, peer in ((1, near), (2, far), (3, cross))
    ]
    for copy in copies:
        copy.start()
    for copy in copies:
        copy.wait()
    return stats[...]


def columns(first, second):
    rows = first.shape[1]
    tall = jnp.concatenate([first, second, jnp.zeros((126, rows), F32)], 0).T
    return tall[:, 0:1], tall[:, 1:2]


def norm_stats(values, stats, sems, base):
    width = values.shape[1]
    local = jnp.sum(values, 1, keepdims=True)
    off = values - local / width
    got = swap_rows((local, jnp.sum(off * off, 1, keepdims=True)), stats, sems, base)
    sums, squares = got[:, 0], got[:, 1]
    mean = jnp.sum(sums, 0, keepdims=True) / D
    shifted = sums / width - mean
    variance = jnp.sum(squares + width * shifted * shifted, 0, keepdims=True) / D
    return columns(mean, lax.rsqrt(variance + 1e-06))


def norm_grad(grad_norm, normed, inverse, stats, sems, base):
    got = swap_rows(
        (jnp.sum(grad_norm, 1, keepdims=True), jnp.sum(grad_norm * normed, 1, keepdims=True)),
        stats,
        sems,
        base,
    )
    total = jnp.sum(got, 0)
    first, second = columns(total[0:1] / D, total[1:2] / D)
    return inverse * (grad_norm - first - normed * second)


def spread(mod, which, rows):
    count = mod.shape[1]
    return jnp.concatenate(
        [
            jnp.broadcast_to(mod[which, l : l + 1], (rows // count, mod.shape[2]))
            for l in range(count)
        ],
        0,
    )


def latent_sums(out, values, which, kinds):
    count = out.shape[0] // kinds
    seq = values.shape[0] // count
    for l in range(count):
        row = l * kinds + which
        out[row : row + 1] = jnp.sum(values[l * seq : (l + 1) * seq], 0, keepdims=True)


def flip(t, *bits):
    for bit in bits:
        t = t + bit * (1 - 2 * ((t // bit) % 2))
    return t


def push_tok(src, dst, sems, at, peer):
    return pltpu.make_async_remote_copy(
        src_ref=src,
        dst_ref=dst,
        send_sem=sems.at[0, at],
        recv_sem=sems.at[1, at],
        device_id={"tok": peer},
        device_id_type=MESH,
    )


def greet_all(count):
    t = lax.axis_index("tok")
    _, near, far, cross = partners()
    barrier = pltpu.get_barrier_semaphore()
    for peer in (near, far, cross):
        pl.semaphore_signal(barrier, inc=1, device_id={"feat": peer}, device_id_type=MESH)
    for step in range(1, count):
        pl.semaphore_signal(
            barrier, inc=1, device_id={"tok": (t + step) % count}, device_id_type=MESH
        )
    pl.semaphore_wait(barrier, FEAT - 1 + count - 1)


def send_all(src, dst, sems, base, count):
    t = lax.axis_index("tok")
    copies = [
        push_tok(src, dst, sems, base + step - 1, (t + step) % count) for step in range(1, count)
    ]
    for copy in copies:
        copy.start()
    return copies


def wait_all(copies):
    for copy in copies:
        copy.wait()


def block_at(ref, block, lead):
    return ref.at[:, block] if lead else ref.at[block]


class RowGather:
    def __init__(self, block, full, lead, order, sems, base):
        t = lax.axis_index("tok")
        self.full, self.lead, self.order, self.sems, self.base = full, lead, list(order), sems, base
        self.held, self.copies = [()], []
        block_at(full, t, lead)[...] = block[...]
        self.send()

    def send(self):
        t = lax.axis_index("tok")
        bit = self.order[0]
        self.copies = []
        for held in self.held:
            view = block_at(self.full, flip(t, *held), self.lead)
            self.copies.append(push_tok(view, view, self.sems, self.base, flip(t, bit)))
            self.base += 1
        for copy in self.copies:
            copy.start()

    def step(self):
        if not self.order:
            return
        wait_all(self.copies)
        bit = self.order.pop(0)
        self.held = self.held + [held + (bit,) for held in self.held]
        if self.order:
            self.send()


class RowScatter:
    def __init__(self, grad, out, acc, recv, lead, order, sems, base):
        self.out, self.acc, self.recv, self.lead = out, acc, recv, lead
        self.order, self.sems, self.base = list(order), sems, base
        t = lax.axis_index("tok")
        self.own = lambda held: block_at(grad, flip(t, *held), lead)
        self.slot = 0
        self.send()

    def send(self):
        t = lax.axis_index("tok")
        bit, rest = self.order[0], self.order[1:]
        self.kept = [()]
        for other in rest:
            self.kept = self.kept + [held + (other,) for held in self.kept]
        self.copies = [
            push_tok(
                self.own((bit,) + held),
                block_at(self.recv, self.slot + at, self.lead),
                self.sems,
                self.base + self.slot + at,
                flip(t, bit),
            )
            for at, held in enumerate(self.kept)
        ]
        for copy in self.copies:
            copy.start()

    def step(self):
        if not self.order:
            return
        places = {}
        for at, held in enumerate(self.kept):
            self.copies[at].wait()
            slot = self.slot + at
            total = self.own(held)[...].astype(F32) + block_at(self.recv, slot, self.lead)[
                ...
            ].astype(F32)
            if len(self.order) == 1:
                self.out[...] = total
            else:
                block_at(self.acc, slot, self.lead)[...] = total.astype(BF16)
            places[frozenset(held)] = slot
        self.slot += len(self.kept)
        self.order.pop(0)
        self.own = lambda held: block_at(self.acc, places[frozenset(held)], self.lead)
        if self.order:
            self.send()


def head_kernel(
    count, orders,
    x, grad_out, cond, ada, bias, qkv, proj, fc1, fc2,
    full, grad_full, normed_out, inverse_out, fc2_sum, mod, cond_all, cond_act, qkv_full, proj_full, fc1_full, fc2_full,
    buf, grad_buf, stats, cond_rows, terms, got, sems, tok_sems,
):
    f, near, far, cross = partners()
    t = lax.axis_index("tok")
    rows, width = x.shape
    lat = cond.shape[0]
    part = ada.shape[1]
    greet_all(count)
    cond_all[t, f] = cond[...]
    shares = [
        push(cond_all.at[t, f], cond_all.at[t, f], sems, at, peer)
        for at, peer in enumerate((near, far, cross))
    ]
    for copy in shares:
        copy.start()
    each = count - 1
    weights = [RowGather(qkv, qkv_full, True, orders[0], tok_sems, 0)]
    wait_all(shares)
    sharing = send_all(cond_all.at[t], cond_all.at[t], tok_sems, 4 * each, count)
    weights.append(RowGather(proj, proj_full, False, orders[1], tok_sems, each))
    weights.append(RowGather(fc1, fc1_full, False, orders[1], tok_sems, 2 * each))
    weights.append(RowGather(fc2, fc2_full, False, orders[0], tok_sems, 3 * each))
    values = x[...]
    mean, inverse = norm_stats(values, stats, sems, 3)
    normed = (values - mean) * inverse
    normed_out[...] = normed
    inverse_out[...] = inverse
    wait_all(sharing)
    picked = jnp.zeros((count * lat, part), F32)
    for block in range(FEAT):
        for owner in range(count):
            cond_rows[block, owner * lat : (owner + 1) * lat] = cond_all[owner, block]
        value = cond_rows[block][:, :width]
        act = (value / (1.0 + jnp.exp(-value))).astype(BF16)
        chosen = (
            lax.broadcasted_iota(jnp.int32, (width, part), 0) + block * width
            == lax.broadcasted_iota(jnp.int32, (width, part), 1) + t * part
        )
        picked += jnp.dot(act, chosen.astype(F32).astype(BF16), preferred_element_type=F32)
    picked = picked.astype(BF16)
    cond_act[...] = picked
    for which in range(6):
        term = jnp.dot(picked, ada[which], preferred_element_type=F32)
        for owner in range(count):
            terms[owner, which] = term[owner * lat : (owner + 1) * lat]
    copies = [
        push_tok(terms.at[(t + step) % count], got.at[step - 1], tok_sems, 5 * each + step - 1, (t + step) % count)
        for step in range(1, count)
    ]
    for copy in copies:
        copy.start()
    for weight in weights:
        weight.step()
    wait_all(copies)
    mod[...] = terms[t] + jnp.sum(got[...], 0) + bias[...]
    mods = mod[...]
    buf[f] = (normed * (1.0 + spread(mods, 1, rows)) + spread(mods, 0, rows)).astype(BF16)
    started = gather_start(buf, sems, 6)
    grad_mlp = (grad_out[...] * spread(mods, 5, rows)).astype(BF16)
    fc2_sum[...] = jnp.sum(grad_mlp.astype(F32), 0, keepdims=True)
    grad_buf[f] = grad_mlp
    grad_started = gather_start(grad_buf, sems, 9)
    for weight in weights:
        weight.step()
    relay = gather_forward(buf, sems, 6, started)
    gather_finish(buf, full, started, relay)
    grad_relay = gather_forward(grad_buf, sems, 9, grad_started)
    gather_finish(grad_buf, grad_full, grad_started, grad_relay)
    for _ in range(count.bit_length()):
        for weight in weights:
            weight.step()


def middle_kernel(
    term, x, mod, bias, attn_out, middle_out, normed_out, inverse_out, full,
    sbuf, near_in, out_buf, far_in, buf, stats, sems,
):
    f, near, far, cross = partners()
    rows = x.shape[0]
    mods = mod[...]
    greet(near, far, cross)
    started = scatter_start(term, sbuf, near_in, sems, 0)
    crossing = scatter_cross(sbuf, near_in, out_buf, far_in, sems, 0, started)
    attn = scatter_finish(sbuf, near_in, far_in, started, crossing) + bias[...]
    attn_out[...] = attn
    middle = x[...] + spread(mods, 2, rows) * attn
    middle_out[...] = middle
    mean, inverse = norm_stats(middle, stats, sems, 3)
    normed = (middle - mean) * inverse
    normed_out[...] = normed
    inverse_out[...] = inverse
    buf[f] = (normed * (1.0 + spread(mods, 4, rows)) + spread(mods, 3, rows)).astype(BF16)
    gathering = gather_start(buf, sems, 6)
    relay = gather_forward(buf, sems, 6, gathering)
    gather_finish(buf, full, gathering, relay)


def back_kernel(
    term, mlp_term, grad_out, normed_in, inverse_in, mod, bias, middle, attn,
    grad_middle_out, full, output, sums, proj_sum,
    sbuf, near_in, out_buf, far_in, mbuf, mnear, mout, mfar, buf, stats, sems,
):
    f, near, far, cross = partners()
    rows = grad_out.shape[0]
    mods = mod[...]
    greet(near, far, cross)
    started = scatter_start(term, sbuf, near_in, sems, 0)
    mlp_started = scatter_start(mlp_term, mbuf, mnear, sems, 3)
    crossing = scatter_cross(sbuf, near_in, out_buf, far_in, sems, 0, started)
    grad_hidden = scatter_finish(sbuf, near_in, far_in, started, crossing)
    normed = normed_in[...]
    grad_middle = grad_out[...] + norm_grad(
        grad_hidden * (1.0 + spread(mods, 4, rows)), normed, inverse_in[...], stats, sems, 6
    )
    grad_attn = (grad_middle * spread(mods, 2, rows)).astype(BF16)
    buf[f] = grad_attn
    gathering = gather_start(buf, sems, 9)
    mlp_crossing = scatter_cross(mbuf, mnear, mout, mfar, sems, 3, mlp_started)
    grad_middle_out[...] = grad_middle
    proj_sum[...] = jnp.sum(grad_attn.astype(F32), 0, keepdims=True)
    latent_sums(sums, grad_hidden, 0, 4)
    latent_sums(sums, grad_hidden * normed, 1, 4)
    latent_sums(sums, grad_middle * attn[...], 2, 4)
    relay = gather_forward(buf, sems, 9, gathering)
    gather_finish(buf, full, gathering, relay)
    mlp_out = scatter_finish(mbuf, mnear, mfar, mlp_started, mlp_crossing) + bias[...]
    output[...] = middle[...] + spread(mods, 5, rows) * mlp_out
    latent_sums(sums, grad_out[...] * mlp_out, 3, 4)


def tail_kernel(
    count, orders,
    term, normed_in, inverse_in, mod, grad_middle, two_sums, ada, biases, fc2, fc1, proj, qkv,
    tokens_grad, grad_mod, cond_terms, bias_sums, fc2_out, fc1_out, proj_out, qkv_out,
    sbuf, near_in, out_buf, far_in, stats, ones, grad_rows, cond_parts, bias_got,
    fc2_acc, fc2_got, fc1_acc, fc1_got, proj_acc, proj_got, qkv_acc, qkv_got, sems, tok_sems,
):
    _, near, far, cross = partners()
    t = lax.axis_index("tok")
    rows = normed_in.shape[0]
    mods = mod[...]
    lat = mods.shape[1]
    each = count - 1
    greet_all(count)
    started = scatter_start(term, sbuf, near_in, sems, 0)
    bias_copies = [
        push_tok(biases, bias_got.at[step - 1], tok_sems, 6 * each + step - 1, (t + step) % count)
        for step in range(1, count)
    ]
    for copy in bias_copies:
        copy.start()
    grads = [
        RowScatter(fc2, fc2_out, fc2_acc, fc2_got, False, orders[0], tok_sems, 0),
        RowScatter(fc1, fc1_out, fc1_acc, fc1_got, False, orders[1], tok_sems, each),
        RowScatter(proj, proj_out, proj_acc, proj_got, False, orders[1], tok_sems, 2 * each),
        RowScatter(qkv, qkv_out, qkv_acc, qkv_got, True, orders[0], tok_sems, 3 * each),
    ]
    crossing = scatter_cross(sbuf, near_in, out_buf, far_in, sems, 0, started)
    grad_hidden = scatter_finish(sbuf, near_in, far_in, started, crossing)
    normed = normed_in[...]
    latent_sums(ones, grad_hidden, 0, 2)
    latent_sums(ones, grad_hidden * normed, 1, 2)
    for l in range(lat):
        one, two = l * 2, l * 4
        kept = (
            ones[one : one + 1],
            ones[one + 1 : one + 2],
            two_sums[two + 2 : two + 3],
            two_sums[two : two + 1],
            two_sums[two + 1 : two + 2],
            two_sums[two + 3 : two + 4],
        )
        for which in range(6):
            grad_mod[t, which, l : l + 1] = kept[which]
    mod_copies = send_all(grad_mod.at[t], grad_mod.at[t], tok_sems, 4 * each, count)
    tokens_grad[...] = grad_middle[...] + norm_grad(
        grad_hidden * (1.0 + spread(mods, 1, rows)), normed, inverse_in[...], stats, sems, 3
    )
    for grad in grads[:2]:
        grad.step()
    wait_all(mod_copies)
    total = None
    for which in range(6):
        for owner in range(count):
            grad_rows[which, owner * lat : (owner + 1) * lat] = grad_mod[owner, which]
        piece = lax.dot_general(
            grad_rows[which].astype(BF16), ada[which], (((1,), (1,)), ((), ())),
            preferred_element_type=F32,
        )
        total = piece if total is None else total + piece
    cond_parts[0] = total
    copies = [
        push(cond_parts.at[0], cond_parts.at[slot], sems, 5 + slot, peer)
        for slot, peer in ((1, near), (2, far), (3, cross))
    ]
    for copy in copies:
        copy.start()
    for grad in grads[2:]:
        grad.step()
    wait_all(copies)
    cond_terms[t] = (cond_parts[0] + cond_parts[1]) + (cond_parts[2] + cond_parts[3])
    cond_copies = send_all(cond_terms.at[t], cond_terms.at[t], tok_sems, 5 * each, count)
    for _ in range(count.bit_length()):
        for grad in grads:
            grad.step()
    wait_all(bias_copies)
    bias_sums[...] = biases[...] + jnp.sum(bias_got[...], 0)
    wait_all(cond_copies)


def call(kernel, collective_id, outs, scratch, sem_counts, *args):
    out_shape = [jax.ShapeDtypeStruct(shape, dtype) for shape, dtype in outs]
    return pl.pallas_call(
        kernel,
        out_shape=out_shape,
        in_specs=[VMEM] * len(args),
        out_specs=[VMEM] * len(outs),
        scratch_shapes=[pltpu.VMEM(shape, dtype) for shape, dtype in scratch]
        + [pltpu.SemaphoreType.DMA((2, count)) for count in sem_counts],
        compiler_params=pltpu.CompilerParams(
            collective_id=collective_id, has_side_effects=True, vmem_limit_bytes=40 * 2**20
        ),
    )(*args)


def per_device(
    tok_count,
    tokens,
    timesteps,
    labels,
    class_table,
    ada_weight,
    ada_bias,
    qkv_weight,
    qv_bias,
    proj_weight,
    proj_bias,
    fc1_weight,
    fc1_bias,
    fc2_weight,
    fc2_bias,
    cotangent,
):
    width, rows = tokens.shape
    lat = timesteps.shape[0]
    seq_len = rows // lat
    head_count = width // HEAD_DIM
    score_scale = HEAD_DIM ** (-0.5)
    feat_at = lax.axis_index("feat")
    offset = feat_at * width
    head_shape = (lat, seq_len, head_count, HEAD_DIM)
    part = ada_weight.shape[1]
    bits = [tok_count >> (i + 1) for i in range(tok_count.bit_length() - 1)]
    gather_orders = (bits, bits[-1:] + bits[:-1])
    scatter_orders = tuple(order[::-1] for order in gather_orders)
    lanes = -(-(width + 1) // 128) * 128
    every = tok_count * lat

    waves = lax.dynamic_slice_in_dim(time_features(timesteps, D), offset, width, 1)
    condition = jnp.take(class_table, labels, axis=1).T.astype(F32) + waves
    own_f32 = ((rows, width), F32)
    own_low = ((rows, width), BF16)
    one_f32 = ((rows, 1), F32)
    full_low = ((rows, D), BF16)
    line = ((1, width), F32)
    buf = ((FEAT, rows, width), BF16)
    stats = ((FEAT, 8, rows), F32)
    scatter_bufs = [buf, ((2, rows, width), BF16), own_low, own_low]

    cond_sent = jnp.concatenate(
        [condition, labels.astype(F32)[:, None], jnp.zeros((lat, lanes - width - 1), F32)], 1
    )
    mod_shape = ((6, lat, width), F32)
    inner = fc1_bias.shape[0]
    small = (tok_count, part, width)
    large = (tok_count, part, inner)
    field_in = tokens.T
    grad_out = cotangent.T
    (
        full_one, grad_mlp_full, normed_one, inverse_one, fc2_bias_grad, mod, cond_all, cond_rows,
        qkv_full, proj_full, fc1_full, fc2_full,
    ) = call(
        partial(head_kernel, tok_count, gather_orders),
        0,
        [
            full_low, full_low, own_f32, one_f32, line, mod_shape,
            ((tok_count, FEAT, lat, lanes), F32), ((every, part), BF16),
            ((3,) + small, BF16), (small, BF16), (large, BF16), (large, BF16),
        ],
        [
            buf, buf, stats, ((FEAT, every, lanes), F32),
            ((tok_count, 6, lat, width), F32), ((tok_count - 1, 6, lat, width), F32),
        ],
        (12, 6 * (tok_count - 1)),
        field_in,
        grad_out,
        cond_sent,
        ada_weight,
        ada_bias[:, None],
        qkv_weight,
        proj_weight,
        fc1_weight,
        fc2_weight,
    )
    qkv_full = qkv_full.reshape(3, D, width)
    proj_full = proj_full.reshape(D, width)
    fc1_full = fc1_full.reshape(D, inner)
    fc2_full = fc2_full.reshape(D, inner)
    cond_all = cond_all.transpose(0, 2, 1, 3).reshape(every, FEAT, lanes)
    labels_all = cond_all[:, 0, width].astype(jnp.int32)
    projected = jnp.einsum("rk,jkc->jrc", full_one, qkv_full, preferred_element_type=F32)
    queries = (projected[0] + qv_bias[0]).astype(BF16).reshape(head_shape)
    keys_low = projected[1].astype(BF16).reshape(head_shape)
    values_low = (projected[2] + qv_bias[1]).astype(BF16).reshape(head_shape)
    scores = (
        jnp.einsum("lqhd,lkhd->lhqk", queries, keys_low, preferred_element_type=F32) * score_scale
    )
    top_score = jnp.max(scores, -1, keepdims=True)
    exponent = jnp.exp(scores - top_score)
    exp_sums = jnp.sum(exponent, -1, keepdims=True)
    probs = exponent / exp_sums
    probs_low = probs.astype(BF16)
    attended = jnp.einsum("lhqk,lkhd->lqhd", probs_low, values_low, preferred_element_type=F32)
    attended = attended.astype(BF16).reshape(rows, width)
    attn_term = jnp.einsum("rc,oc->ro", attended, proj_full, preferred_element_type=F32)
    attn_out, middle, normed_two, inverse_two, full_two = call(
        middle_kernel,
        2,
        [own_f32, own_f32, own_f32, one_f32, full_low],
        scatter_bufs + [buf, stats],
        (9,),
        attn_term.astype(BF16),
        field_in,
        mod,
        proj_bias[None],
    )
    pre_act = jnp.dot(full_two, fc1_full, preferred_element_type=F32) + fc1_bias
    act_value, gelu_back = jax.vjp(partial(jax.nn.gelu, approximate=True), pre_act)
    act_low = act_value.astype(BF16)
    grad_act = jnp.dot(grad_mlp_full, fc2_full, preferred_element_type=F32)
    grad_pre = gelu_back(grad_act)[0].astype(BF16)
    mlp_term = jnp.einsum("rf,of->ro", act_low, fc2_full, preferred_element_type=F32)
    hidden_two_term = jnp.einsum("rf,kf->rk", grad_pre, fc1_full, preferred_element_type=F32)
    grad_middle, grad_attn_full, output, two_sums, proj_bias_grad = call(
        back_kernel,
        3,
        [own_f32, full_low, own_f32, ((lat * 4, width), F32), line],
        scatter_bufs + scatter_bufs + [buf, stats],
        (12,),
        hidden_two_term.astype(BF16),
        mlp_term.astype(BF16),
        grad_out,
        normed_two,
        inverse_two,
        mod,
        fc2_bias[None],
        middle,
        attn_out,
    )
    fc2_grad = jnp.einsum("ro,rf->of", grad_mlp_full, act_low, preferred_element_type=F32)
    fc1_bias_grad = jnp.sum(grad_pre, 0, dtype=F32)
    fc1_grad = jnp.einsum("rk,rf->kf", full_two, grad_pre, preferred_element_type=F32)
    proj_grad = jnp.einsum("ro,rc->oc", grad_attn_full, attended, preferred_element_type=F32)
    grad_attended = (
        jnp.dot(grad_attn_full, proj_full, preferred_element_type=F32)
        .astype(BF16)
        .reshape(head_shape)
    )
    grad_values = jnp.einsum(
        "lhqk,lqhd->lkhd", probs_low, grad_attended, preferred_element_type=F32
    )
    grad_probs = jnp.einsum(
        "lqhd,lkhd->lhqk", grad_attended, values_low, preferred_element_type=F32
    )
    grad_scores = (
        probs * (grad_probs - jnp.sum(grad_probs * probs, -1, keepdims=True))
    ).astype(BF16)
    grad_queries = (
        jnp.einsum("lhqk,lkhd->lqhd", grad_scores, keys_low, preferred_element_type=F32)
        * score_scale
    )
    grad_keys = (
        jnp.einsum("lhqk,lqhd->lkhd", grad_scores, queries, preferred_element_type=F32)
        * score_scale
    )
    grad_qkv = (
        jnp.stack([grad_queries, grad_keys, grad_values]).astype(BF16).reshape(3, rows, width)
    )
    hidden_one_term = jnp.einsum("jrc,jkc->rk", grad_qkv, qkv_full, preferred_element_type=F32)
    qkv_grad = jnp.einsum("rk,jrc->jkc", full_one, grad_qkv, preferred_element_type=F32)
    bias_terms = jnp.concatenate(
        [
            jnp.sum(grad_qkv[0], 0, dtype=F32)[None],
            jnp.sum(grad_qkv[2], 0, dtype=F32)[None],
            proj_bias_grad,
            fc1_bias_grad.reshape(-1, width),
            fc2_bias_grad,
        ]
    )
    small_parts = [((tok_count - 1, part, width), BF16)] * 2
    large_parts = [((tok_count - 1, part, inner), BF16)] * 2
    (
        tokens_grad, grad_mod_all, cond_terms, bias_sums, fc2_shard, fc1_shard, proj_shard, qkv_shard
    ) = call(
        partial(tail_kernel, tok_count, scatter_orders),
        4,
        [
            own_f32, ((tok_count, 6, lat, width), F32), ((tok_count, every, part), F32),
            (bias_terms.shape, F32),
            ((part, inner), F32), ((part, inner), F32), ((part, width), F32), ((3, part, width), F32),
        ],
        scatter_bufs
        + [
            stats, ((lat * 2, width), F32), ((6, every, width), F32), ((FEAT, every, part), F32),
            ((tok_count - 1,) + bias_terms.shape, F32),
        ]
        + large_parts + large_parts + small_parts
        + [((3, tok_count - 1, part, width), BF16)] * 2,
        (9, 7 * (tok_count - 1)),
        hidden_one_term.astype(BF16),
        normed_one,
        inverse_one,
        mod,
        grad_middle,
        two_sums,
        ada_weight,
        bias_terms,
        fc2_grad.astype(BF16).reshape(large),
        fc1_grad.astype(BF16).reshape(large),
        proj_grad.astype(BF16).reshape(small),
        qkv_grad.astype(BF16).reshape((3,) + small),
    )
    grad_mod_all = grad_mod_all.astype(BF16)
    ada_bias_sum = jnp.sum(grad_mod_all, (0, 2), dtype=F32)
    grad_mod_all = grad_mod_all.transpose(0, 2, 1, 3).reshape(every, 6, width)
    ada_shard = jnp.einsum("lk,ljc->jkc", cond_rows, grad_mod_all, preferred_element_type=F32)
    grad_cond_act = cond_terms.transpose(1, 0, 2).reshape(every, D)
    own_cond = lax.dynamic_index_in_dim(cond_all, feat_at, 1, False)[:, :width]
    own_grad = lax.dynamic_slice_in_dim(grad_cond_act, offset, width, 1)
    grad_condition = jax.vjp(jax.nn.silu, own_cond)[1](own_grad)[0]
    class_count = class_table.shape[1]
    one_hot = (
        labels_all[:, None] == jnp.arange(class_count, dtype=jnp.int32)[None, :]
    ).astype(F32)
    class_sum = jnp.einsum("lc,lw->wc", one_hot, grad_condition, precision=lax.Precision.HIGHEST)
    return (
        output.T,
        tokens_grad.T,
        class_sum,
        ada_shard,
        ada_bias_sum,
        qkv_shard,
        bias_sums[:2],
        proj_shard,
        bias_sums[2],
        fc1_shard,
        bias_sums[3:-1].reshape(-1),
        fc2_shard,
        bias_sums[-1],
    )


def solution(mesh):
    return jax.shard_map(
        partial(per_device, mesh.shape["tok"]),
        mesh=mesh,
        in_specs=(
            P("feat", "tok"),
            P("tok"),
            P("tok"),
            P("feat", None),
            P(None, "tok", "feat"),
            P(None, "feat"),
            P(None, "tok", "feat"),
            P(None, "feat"),
            P("tok", "feat"),
            P("feat"),
            P("tok", "feat"),
            P("feat"),
            P("tok", "feat"),
            P("feat"),
            P("feat", "tok"),
        ),
        out_specs=(
            P("feat", "tok"),
            P("feat", "tok"),
            P("feat", None),
            P(None, "tok", "feat"),
            P(None, "feat"),
            P(None, "tok", "feat"),
            P(None, "feat"),
            P("tok", "feat"),
            P("feat"),
            P("tok", "feat"),
            P("feat"),
            P("tok", "feat"),
            P("feat"),
        ),
        check_vma=False,
    )
```

```python
from functools import partial
import math

import jax
import jax.numpy as jnp
from jax import lax
from jax.experimental import pallas as pl
from jax.experimental.pallas import tpu as pltpu
from jax.sharding import PartitionSpec as P

D = 768
HEAD_DIM = 64
FEAT = 4
MESH = pl.DeviceIdType.MESH
F32 = jnp.float32
BF16 = jnp.bfloat16
VMEM = pl.BlockSpec(memory_space=pltpu.VMEM)


def time_features(step_ids, feat_count):
    half_width = feat_count // 2
    frequency = jnp.exp(-math.log(10000.0) * jnp.arange(half_width, dtype=jnp.float32) / half_width)
    angles = step_ids.astype(jnp.float32)[:, None] * frequency[None, :]
    return jnp.concatenate([jnp.cos(angles), jnp.sin(angles)], axis=-1)


def partners():
    f = lax.axis_index("feat")
    near = f + 1 - 2 * (f % 2)
    far = (f + 2) % FEAT
    return f, near, far, (near + 2) % FEAT


def greet(near, far, cross):
    barrier = pltpu.get_barrier_semaphore()
    for peer in (near, far, cross):
        pl.semaphore_signal(barrier, inc=1, device_id={"feat": peer}, device_id_type=MESH)
    pl.semaphore_wait(barrier, 3)


def push(src, dst, sems, at, peer):
    return pltpu.make_async_remote_copy(
        src_ref=src,
        dst_ref=dst,
        send_sem=sems.at[0, at],
        recv_sem=sems.at[1, at],
        device_id={"feat": peer},
        device_id_type=MESH,
    )


def gather_start(buf, sems, base):
    f, near, far, _ = partners()
    to_far = push(buf.at[f], buf.at[f], sems, base, far)
    to_near = push(buf.at[f], buf.at[f], sems, base + 1, near)
    to_far.start()
    to_near.start()
    return to_far, to_near


def gather_forward(buf, sems, base, started):
    _, near, far, _ = partners()
    started[0].wait_recv()
    relay = push(buf.at[far], buf.at[far], sems, base + 2, near)
    relay.start()
    return relay


def gather_finish(buf, out, started, relay):
    started[1].wait_recv()
    relay.wait_recv()
    for copy in (*started, relay):
        copy.wait_send()
    width = buf.shape[2]
    for block in range(FEAT):
        out[:, block * width : (block + 1) * width] = buf[block]


def scatter_start(term, buf, near_in, sems, base):
    f, near, _, _ = partners()
    side, core = f // 2, f % 2
    width = buf.shape[2]
    for block in range(FEAT):
        buf[block] = term[:, block * width : (block + 1) * width]
    first = push(buf.at[2 * (1 - side) + 1 - core], near_in.at[0], sems, base, near)
    second = push(buf.at[2 * side + 1 - core], near_in.at[1], sems, base + 1, near)
    first.start()
    second.start()
    return first, second


def scatter_cross(buf, near_in, out_buf, far_in, sems, base, started):
    _, _, far, _ = partners()
    started[0].wait_recv()
    out_buf[...] = (buf[far].astype(F32) + near_in[0].astype(F32)).astype(BF16)
    cross = push(out_buf, far_in, sems, base + 2, far)
    cross.start()
    return cross


def scatter_finish(buf, near_in, far_in, started, cross):
    f, _, _, _ = partners()
    started[1].wait_recv()
    own = buf[f].astype(F32) + near_in[1].astype(F32)
    cross.wait_recv()
    for copy in (*started, cross):
        copy.wait_send()
    return own + far_in[...].astype(F32)


def swap_rows(pair, stats, sems, base):
    _, near, far, cross = partners()
    rows = pair[0].shape[0]
    lane = lax.broadcasted_iota(jnp.int32, (rows, 128), 1)
    packed = jnp.where(lane == 0, pair[0], jnp.where(lane == 1, pair[1], 0.0))
    stats[0] = packed.T[:8]
    copies = [
        push(stats.at[0], stats.at[slot], sems, base + slot - 1, peer)
        for slot, peer in ((1, near), (2, far), (3, cross))
    ]
    for copy in copies:
        copy.start()
    for copy in copies:
        copy.wait()
    return stats[...]


def columns(first, second):
    rows = first.shape[1]
    tall = jnp.concatenate([first, second, jnp.zeros((126, rows), F32)], 0).T
    return tall[:, 0:1], tall[:, 1:2]


def norm_stats(values, stats, sems, base):
    width = values.shape[1]
    local = jnp.sum(values, 1, keepdims=True)
    off = values - local / width
    got = swap_rows((local, jnp.sum(off * off, 1, keepdims=True)), stats, sems, base)
    sums, squares = got[:, 0], got[:, 1]
    mean = jnp.sum(sums, 0, keepdims=True) / D
    shifted = sums / width - mean
    variance = jnp.sum(squares + width * shifted * shifted, 0, keepdims=True) / D
    return columns(mean, lax.rsqrt(variance + 1e-06))


def norm_grad(grad_norm, normed, inverse, stats, sems, base):
    got = swap_rows(
        (jnp.sum(grad_norm, 1, keepdims=True), jnp.sum(grad_norm * normed, 1, keepdims=True)),
        stats,
        sems,
        base,
    )
    total = jnp.sum(got, 0)
    first, second = columns(total[0:1] / D, total[1:2] / D)
    return inverse * (grad_norm - first - normed * second)


def spread(mod, which, rows):
    count = mod.shape[1]
    return jnp.concatenate(
        [
            jnp.broadcast_to(mod[which, l : l + 1], (rows // count, mod.shape[2]))
            for l in range(count)
        ],
        0,
    )


def latent_sums(out, values, which, kinds):
    count = out.shape[0] // kinds
    seq = values.shape[0] // count
    for l in range(count):
        row = l * kinds + which
        out[row : row + 1] = jnp.sum(values[l * seq : (l + 1) * seq], 0, keepdims=True)


def flip(t, *bits):
    for bit in bits:
        t = t + bit * (1 - 2 * ((t // bit) % 2))
    return t


def push_tok(src, dst, sems, at, peer):
    return pltpu.make_async_remote_copy(
        src_ref=src,
        dst_ref=dst,
        send_sem=sems.at[0, at],
        recv_sem=sems.at[1, at],
        device_id={"tok": peer},
        device_id_type=MESH,
    )


def greet_all(count):
    t = lax.axis_index("tok")
    _, near, far, cross = partners()
    barrier = pltpu.get_barrier_semaphore()
    for peer in (near, far, cross):
        pl.semaphore_signal(barrier, inc=1, device_id={"feat": peer}, device_id_type=MESH)
    for step in range(1, count):
        pl.semaphore_signal(
            barrier, inc=1, device_id={"tok": (t + step) % count}, device_id_type=MESH
        )
    pl.semaphore_wait(barrier, FEAT - 1 + count - 1)


def send_all(src, dst, sems, base, count):
    t = lax.axis_index("tok")
    copies = [
        push_tok(src, dst, sems, base + step - 1, (t + step) % count) for step in range(1, count)
    ]
    for copy in copies:
        copy.start()
    return copies


def wait_all(copies):
    for copy in copies:
        copy.wait()


def block_at(ref, block, lead, cols=None):
    if cols is not None:
        return ref.at[block, :, cols]
    return ref.at[:, block] if lead else ref.at[block]


def halves(ref):
    half = ref.shape[-1] // 2
    return pl.ds(0, half), pl.ds(half, half)


class RowGather:
    def __init__(self, block, full, lead, order, sems, base, cols=None):
        t = lax.axis_index("tok")
        self.full, self.lead, self.order, self.sems, self.base = full, lead, list(order), sems, base
        self.held, self.copies, self.cols = [()], [], cols
        block_at(full, t, lead, cols)[...] = block[...] if cols is None else block[:, cols]
        self.send()

    def send(self):
        t = lax.axis_index("tok")
        bit = self.order[0]
        self.copies = []
        for held in self.held:
            view = block_at(self.full, flip(t, *held), self.lead, self.cols)
            self.copies.append(push_tok(view, view, self.sems, self.base, flip(t, bit)))
            self.base += 1
        for copy in self.copies:
            copy.start()

    def step(self):
        if not self.order:
            return
        wait_all(self.copies)
        bit = self.order.pop(0)
        self.held = self.held + [held + (bit,) for held in self.held]
        if self.order:
            self.send()


class RowScatter:
    def __init__(self, grad, out, acc, recv, lead, order, sems, base, cols=None):
        self.out, self.acc, self.recv, self.lead = out, acc, recv, lead
        self.cols = cols
        self.order, self.sems, self.base = list(order), sems, base
        t = lax.axis_index("tok")
        self.own = lambda held: block_at(grad, flip(t, *held), lead, cols)
        self.slot = 0
        self.send()

    def send(self):
        t = lax.axis_index("tok")
        bit, rest = self.order[0], self.order[1:]
        self.kept = [()]
        for other in rest:
            self.kept = self.kept + [held + (other,) for held in self.kept]
        self.copies = [
            push_tok(
                self.own((bit,) + held),
                block_at(self.recv, self.slot + at, self.lead, self.cols),
                self.sems,
                self.base + self.slot + at,
                flip(t, bit),
            )
            for at, held in enumerate(self.kept)
        ]
        for copy in self.copies:
            copy.start()

    def step(self):
        if not self.order:
            return
        places = {}
        for at, held in enumerate(self.kept):
            self.copies[at].wait()
            slot = self.slot + at
            total = self.own(held)[...].astype(F32) + block_at(
                self.recv, slot, self.lead, self.cols
            )[...].astype(F32)
            if len(self.order) == 1 and self.cols is None:
                self.out[...] = total
            elif len(self.order) == 1:
                self.out[:, self.cols] = total
            else:
                block_at(self.acc, slot, self.lead, self.cols)[...] = total.astype(BF16)
            places[frozenset(held)] = slot
        self.slot += len(self.kept)
        self.order.pop(0)
        self.own = lambda held: block_at(
            self.acc, places[frozenset(held)], self.lead, self.cols
        )
        if self.order:
            self.send()


def head_kernel(
    count, orders,
    x, grad_out, cond, ada, bias, qkv, proj, fc1,
    full, grad_full, normed_out, inverse_out, fc2_sum, mod, cond_all, cond_act, qkv_full, proj_full, fc1_full,
    buf, grad_buf, stats, cond_rows, terms, got, sems, tok_sems,
):
    f, near, far, cross = partners()
    t = lax.axis_index("tok")
    rows, width = x.shape
    lat = cond.shape[0]
    part = ada.shape[1]
    greet_all(count)
    cond_all[t, f] = cond[...]
    shares = [
        push(cond_all.at[t, f], cond_all.at[t, f], sems, at, peer)
        for at, peer in enumerate((near, far, cross))
    ]
    for copy in shares:
        copy.start()
    each = count - 1
    weights = [RowGather(qkv, qkv_full, True, orders[0], tok_sems, 0)]
    wait_all(shares)
    sharing = send_all(cond_all.at[t], cond_all.at[t], tok_sems, 4 * each, count)
    weights.append(RowGather(proj, proj_full, False, orders[1], tok_sems, each))
    for at, cols in enumerate(halves(fc1)):
        weights.append(
            RowGather(fc1, fc1_full, False, orders[1 - at], tok_sems, (2 + at) * each, cols)
        )
    values = x[...]
    mean, inverse = norm_stats(values, stats, sems, 3)
    normed = (values - mean) * inverse
    normed_out[...] = normed
    inverse_out[...] = inverse
    wait_all(sharing)
    picked = jnp.zeros((count * lat, part), F32)
    for block in range(FEAT):
        for owner in range(count):
            cond_rows[block, owner * lat : (owner + 1) * lat] = cond_all[owner, block]
        value = cond_rows[block][:, :width]
        act = (value / (1.0 + jnp.exp(-value))).astype(BF16)
        chosen = (
            lax.broadcasted_iota(jnp.int32, (width, part), 0) + block * width
            == lax.broadcasted_iota(jnp.int32, (width, part), 1) + t * part
        )
        picked += jnp.dot(act, chosen.astype(F32).astype(BF16), preferred_element_type=F32)
    picked = picked.astype(BF16)
    cond_act[...] = picked
    for which in range(6):
        term = jnp.dot(picked, ada[which], preferred_element_type=F32)
        for owner in range(count):
            terms[owner, which] = term[owner * lat : (owner + 1) * lat]
    copies = [
        push_tok(terms.at[(t + step) % count], got.at[step - 1], tok_sems, 5 * each + step - 1, (t + step) % count)
        for step in range(1, count)
    ]
    for copy in copies:
        copy.start()
    for weight in weights:
        weight.step()
    wait_all(copies)
    mod[...] = terms[t] + jnp.sum(got[...], 0) + bias[...]
    mods = mod[...]
    buf[f] = (normed * (1.0 + spread(mods, 1, rows)) + spread(mods, 0, rows)).astype(BF16)
    started = gather_start(buf, sems, 6)
    grad_mlp = (grad_out[...] * spread(mods, 5, rows)).astype(BF16)
    fc2_sum[...] = jnp.sum(grad_mlp.astype(F32), 0, keepdims=True)
    grad_buf[f] = grad_mlp
    grad_started = gather_start(grad_buf, sems, 9)
    for weight in weights:
        weight.step()
    relay = gather_forward(buf, sems, 6, started)
    gather_finish(buf, full, started, relay)
    grad_relay = gather_forward(grad_buf, sems, 9, grad_started)
    gather_finish(grad_buf, grad_full, grad_started, grad_relay)
    for _ in range(count.bit_length()):
        for weight in weights:
            weight.step()


def middle_kernel(
    count, orders,
    term, x, mod, bias, fc2, fc2_full, attn_out, middle_out, normed_out, inverse_out, full,
    sbuf, near_in, out_buf, far_in, buf, stats, sems, tok_sems,
):
    f, near, far, cross = partners()
    rows = x.shape[0]
    mods = mod[...]
    greet_all(count)
    started = scatter_start(term, sbuf, near_in, sems, 0)
    weights = [
        RowGather(fc2, fc2_full, False, orders[1 - at], tok_sems, at * (count - 1), cols)
        for at, cols in enumerate(halves(fc2))
    ]
    crossing = scatter_cross(sbuf, near_in, out_buf, far_in, sems, 0, started)
    attn = scatter_finish(sbuf, near_in, far_in, started, crossing) + bias[...]
    attn_out[...] = attn
    for weight in weights:
        weight.step()
    middle = x[...] + spread(mods, 2, rows) * attn
    middle_out[...] = middle
    mean, inverse = norm_stats(middle, stats, sems, 3)
    normed = (middle - mean) * inverse
    normed_out[...] = normed
    inverse_out[...] = inverse
    buf[f] = (normed * (1.0 + spread(mods, 4, rows)) + spread(mods, 3, rows)).astype(BF16)
    gathering = gather_start(buf, sems, 6)
    for weight in weights:
        weight.step()
    relay = gather_forward(buf, sems, 6, gathering)
    gather_finish(buf, full, gathering, relay)
    for _ in range(count.bit_length()):
        for weight in weights:
            weight.step()


def back_kernel(
    count, orders,
    term, mlp_term, grad_out, normed_in, inverse_in, mod, bias, middle, attn, fc2,
    fc2_out, grad_middle_out, full, output, sums, proj_sum,
    sbuf, near_in, out_buf, far_in, mbuf, mnear, mout, mfar, buf, stats, fc2_acc, fc2_got, sems, tok_sems,
):
    f, near, far, cross = partners()
    rows = grad_out.shape[0]
    mods = mod[...]
    greet_all(count)
    started = scatter_start(term, sbuf, near_in, sems, 0)
    grads = [
        RowScatter(
            fc2, fc2_out, fc2_acc, fc2_got, False, orders[at], tok_sems, at * (count - 1), cols
        )
        for at, cols in enumerate(halves(fc2))
    ]
    mlp_started = scatter_start(mlp_term, mbuf, mnear, sems, 3)
    crossing = scatter_cross(sbuf, near_in, out_buf, far_in, sems, 0, started)
    grad_hidden = scatter_finish(sbuf, near_in, far_in, started, crossing)
    normed = normed_in[...]
    grad_middle = grad_out[...] + norm_grad(
        grad_hidden * (1.0 + spread(mods, 4, rows)), normed, inverse_in[...], stats, sems, 6
    )
    grad_attn = (grad_middle * spread(mods, 2, rows)).astype(BF16)
    buf[f] = grad_attn
    gathering = gather_start(buf, sems, 9)
    mlp_crossing = scatter_cross(mbuf, mnear, mout, mfar, sems, 3, mlp_started)
    for grad in grads:
        grad.step()
    grad_middle_out[...] = grad_middle
    proj_sum[...] = jnp.sum(grad_attn.astype(F32), 0, keepdims=True)
    latent_sums(sums, grad_hidden, 0, 4)
    latent_sums(sums, grad_hidden * normed, 1, 4)
    latent_sums(sums, grad_middle * attn[...], 2, 4)
    relay = gather_forward(buf, sems, 9, gathering)
    gather_finish(buf, full, gathering, relay)
    for grad in grads:
        grad.step()
    mlp_out = scatter_finish(mbuf, mnear, mfar, mlp_started, mlp_crossing) + bias[...]
    output[...] = middle[...] + spread(mods, 5, rows) * mlp_out
    latent_sums(sums, grad_out[...] * mlp_out, 3, 4)
    for _ in range(count.bit_length()):
        for grad in grads:
            grad.step()


def tail_kernel(
    count, orders,
    term, normed_in, inverse_in, mod, grad_middle, two_sums, ada, biases, fc1, proj, qkv,
    tokens_grad, grad_mod, cond_terms, bias_sums, fc1_out, proj_out, qkv_out,
    sbuf, near_in, out_buf, far_in, stats, ones, grad_rows, cond_parts, bias_got,
    fc1_acc, fc1_got, proj_acc, proj_got, qkv_acc, qkv_got, sems, tok_sems,
):
    _, near, far, cross = partners()
    t = lax.axis_index("tok")
    rows = normed_in.shape[0]
    mods = mod[...]
    lat = mods.shape[1]
    each = count - 1
    greet_all(count)
    started = scatter_start(term, sbuf, near_in, sems, 0)
    bias_copies = [
        push_tok(biases, bias_got.at[step - 1], tok_sems, 6 * each + step - 1, (t + step) % count)
        for step in range(1, count)
    ]
    for copy in bias_copies:
        copy.start()
    grads = [
        RowScatter(fc1, fc1_out, fc1_acc, fc1_got, False, orders[at], tok_sems, at * each, cols)
        for at, cols in enumerate(halves(fc1))
    ] + [
        RowScatter(proj, proj_out, proj_acc, proj_got, False, orders[1], tok_sems, 2 * each),
        RowScatter(qkv, qkv_out, qkv_acc, qkv_got, True, orders[0], tok_sems, 3 * each),
    ]
    crossing = scatter_cross(sbuf, near_in, out_buf, far_in, sems, 0, started)
    grad_hidden = scatter_finish(sbuf, near_in, far_in, started, crossing)
    normed = normed_in[...]
    latent_sums(ones, grad_hidden, 0, 2)
    latent_sums(ones, grad_hidden * normed, 1, 2)
    for l in range(lat):
        one, two = l * 2, l * 4
        kept = (
            ones[one : one + 1],
            ones[one + 1 : one + 2],
            two_sums[two + 2 : two + 3],
            two_sums[two : two + 1],
            two_sums[two + 1 : two + 2],
            two_sums[two + 3 : two + 4],
        )
        for which in range(6):
            grad_mod[t, which, l : l + 1] = kept[which]
    mod_copies = send_all(grad_mod.at[t], grad_mod.at[t], tok_sems, 4 * each, count)
    tokens_grad[...] = grad_middle[...] + norm_grad(
        grad_hidden * (1.0 + spread(mods, 1, rows)), normed, inverse_in[...], stats, sems, 3
    )
    for grad in grads[:2]:
        grad.step()
    wait_all(mod_copies)
    total = None
    for which in range(6):
        for owner in range(count):
            grad_rows[which, owner * lat : (owner + 1) * lat] = grad_mod[owner, which]
        piece = lax.dot_general(
            grad_rows[which].astype(BF16), ada[which], (((1,), (1,)), ((), ())),
            preferred_element_type=F32,
        )
        total = piece if total is None else total + piece
    cond_parts[0] = total
    copies = [
        push(cond_parts.at[0], cond_parts.at[slot], sems, 5 + slot, peer)
        for slot, peer in ((1, near), (2, far), (3, cross))
    ]
    for copy in copies:
        copy.start()
    for grad in grads[2:]:
        grad.step()
    wait_all(copies)
    cond_terms[t] = (cond_parts[0] + cond_parts[1]) + (cond_parts[2] + cond_parts[3])
    cond_copies = send_all(cond_terms.at[t], cond_terms.at[t], tok_sems, 5 * each, count)
    for _ in range(count.bit_length()):
        for grad in grads:
            grad.step()
    wait_all(bias_copies)
    bias_sums[...] = biases[...] + jnp.sum(bias_got[...], 0)
    wait_all(cond_copies)


def call(kernel, collective_id, outs, scratch, sem_counts, *args):
    out_shape = [jax.ShapeDtypeStruct(shape, dtype) for shape, dtype in outs]
    return pl.pallas_call(
        kernel,
        out_shape=out_shape,
        in_specs=[VMEM] * len(args),
        out_specs=[VMEM] * len(outs),
        scratch_shapes=[pltpu.VMEM(shape, dtype) for shape, dtype in scratch]
        + [pltpu.SemaphoreType.DMA((2, count)) for count in sem_counts],
        compiler_params=pltpu.CompilerParams(
            collective_id=collective_id, has_side_effects=True, vmem_limit_bytes=40 * 2**20
        ),
    )(*args)


def per_device(
    tok_count,
    tokens,
    timesteps,
    labels,
    class_table,
    ada_weight,
    ada_bias,
    qkv_weight,
    qv_bias,
    proj_weight,
    proj_bias,
    fc1_weight,
    fc1_bias,
    fc2_weight,
    fc2_bias,
    cotangent,
):
    width, rows = tokens.shape
    lat = timesteps.shape[0]
    seq_len = rows // lat
    head_count = width // HEAD_DIM
    score_scale = HEAD_DIM ** (-0.5)
    feat_at = lax.axis_index("feat")
    offset = feat_at * width
    head_shape = (lat, seq_len, head_count, HEAD_DIM)
    part = ada_weight.shape[1]
    bits = [tok_count >> (i + 1) for i in range(tok_count.bit_length() - 1)]
    gather_orders = (bits, bits[-1:] + bits[:-1])
    scatter_orders = tuple(order[::-1] for order in gather_orders)
    lanes = -(-(width + 1) // 128) * 128
    every = tok_count * lat

    waves = lax.dynamic_slice_in_dim(time_features(timesteps, D), offset, width, 1)
    condition = jnp.take(class_table, labels, axis=1).T.astype(F32) + waves
    own_f32 = ((rows, width), F32)
    own_low = ((rows, width), BF16)
    one_f32 = ((rows, 1), F32)
    full_low = ((rows, D), BF16)
    line = ((1, width), F32)
    buf = ((FEAT, rows, width), BF16)
    stats = ((FEAT, 8, rows), F32)
    scatter_bufs = [buf, ((2, rows, width), BF16), own_low, own_low]

    cond_sent = jnp.concatenate(
        [condition, labels.astype(F32)[:, None], jnp.zeros((lat, lanes - width - 1), F32)], 1
    )
    mod_shape = ((6, lat, width), F32)
    inner = fc1_bias.shape[0]
    small = (tok_count, part, width)
    large = (tok_count, part, inner)
    small_parts = [((tok_count - 1, part, width), BF16)] * 2
    large_parts = [((tok_count - 1, part, inner), BF16)] * 2
    field_in = tokens.T
    grad_out = cotangent.T
    (
        full_one, grad_mlp_full, normed_one, inverse_one, fc2_bias_grad, mod, cond_all, cond_rows,
        qkv_full, proj_full, fc1_full,
    ) = call(
        partial(head_kernel, tok_count, gather_orders),
        0,
        [
            full_low, full_low, own_f32, one_f32, line, mod_shape,
            ((tok_count, FEAT, lat, lanes), F32), ((every, part), BF16),
            ((3,) + small, BF16), (small, BF16), (large, BF16),
        ],
        [
            buf, buf, stats, ((FEAT, every, lanes), F32),
            ((tok_count, 6, lat, width), F32), ((tok_count - 1, 6, lat, width), F32),
        ],
        (12, 6 * (tok_count - 1)),
        field_in,
        grad_out,
        cond_sent,
        ada_weight,
        ada_bias[:, None],
        qkv_weight,
        proj_weight,
        fc1_weight,
    )
    qkv_full = qkv_full.reshape(3, D, width)
    proj_full = proj_full.reshape(D, width)
    fc1_full = fc1_full.reshape(D, inner)
    cond_all = cond_all.transpose(0, 2, 1, 3).reshape(every, FEAT, lanes)
    labels_all = cond_all[:, 0, width].astype(jnp.int32)
    projected = jnp.einsum("rk,jkc->jrc", full_one, qkv_full, preferred_element_type=F32)
    queries = (projected[0] + qv_bias[0]).astype(BF16).reshape(head_shape)
    keys_low = projected[1].astype(BF16).reshape(head_shape)
    values_low = (projected[2] + qv_bias[1]).astype(BF16).reshape(head_shape)
    scores = (
        jnp.einsum("lqhd,lkhd->lhqk", queries, keys_low, preferred_element_type=F32) * score_scale
    )
    top_score = jnp.max(scores, -1, keepdims=True)
    exponent = jnp.exp(scores - top_score)
    exp_sums = jnp.sum(exponent, -1, keepdims=True)
    probs = exponent / exp_sums
    probs_low = probs.astype(BF16)
    attended = jnp.einsum("lhqk,lkhd->lqhd", probs_low, values_low, preferred_element_type=F32)
    attended = attended.astype(BF16).reshape(rows, width)
    attn_term = jnp.einsum("rc,oc->ro", attended, proj_full, preferred_element_type=F32)
    fc2_full, attn_out, middle, normed_two, inverse_two, full_two = call(
        partial(middle_kernel, tok_count, gather_orders),
        2,
        [(large, BF16), own_f32, own_f32, own_f32, one_f32, full_low],
        scatter_bufs + [buf, stats],
        (9, 2 * (tok_count - 1)),
        attn_term.astype(BF16),
        field_in,
        mod,
        proj_bias[None],
        fc2_weight,
    )
    fc2_full = fc2_full.reshape(D, inner)
    pre_act = jnp.dot(full_two, fc1_full, preferred_element_type=F32) + fc1_bias
    act_value, gelu_back = jax.vjp(partial(jax.nn.gelu, approximate=True), pre_act)
    act_low = act_value.astype(BF16)
    grad_act = jnp.dot(grad_mlp_full, fc2_full, preferred_element_type=F32)
    grad_pre = gelu_back(grad_act)[0].astype(BF16)
    mlp_term = jnp.einsum("rf,of->ro", act_low, fc2_full, preferred_element_type=F32)
    hidden_two_term = jnp.einsum("rf,kf->rk", grad_pre, fc1_full, preferred_element_type=F32)
    fc2_grad = jnp.einsum("ro,rf->of", grad_mlp_full, act_low, preferred_element_type=F32)
    fc2_shard, grad_middle, grad_attn_full, output, two_sums, proj_bias_grad = call(
        partial(back_kernel, tok_count, scatter_orders),
        3,
        [((part, inner), F32), own_f32, full_low, own_f32, ((lat * 4, width), F32), line],
        scatter_bufs + scatter_bufs + [buf, stats] + large_parts,
        (12, 2 * (tok_count - 1)),
        hidden_two_term.astype(BF16),
        mlp_term.astype(BF16),
        grad_out,
        normed_two,
        inverse_two,
        mod,
        fc2_bias[None],
        middle,
        attn_out,
        fc2_grad.astype(BF16).reshape(large),
    )
    fc1_bias_grad = jnp.sum(grad_pre, 0, dtype=F32)
    fc1_grad = jnp.einsum("rk,rf->kf", full_two, grad_pre, preferred_element_type=F32)
    proj_grad = jnp.einsum("ro,rc->oc", grad_attn_full, attended, preferred_element_type=F32)
    grad_attended = (
        jnp.dot(grad_attn_full, proj_full, preferred_element_type=F32)
        .astype(BF16)
        .reshape(head_shape)
    )
    grad_values = jnp.einsum(
        "lhqk,lqhd->lkhd", probs_low, grad_attended, preferred_element_type=F32
    )
    grad_probs = jnp.einsum(
        "lqhd,lkhd->lhqk", grad_attended, values_low, preferred_element_type=F32
    )
    grad_scores = (
        probs * (grad_probs - jnp.sum(grad_probs * probs, -1, keepdims=True))
    ).astype(BF16)
    grad_queries = (
        jnp.einsum("lhqk,lkhd->lqhd", grad_scores, keys_low, preferred_element_type=F32)
        * score_scale
    )
    grad_keys = (
        jnp.einsum("lhqk,lqhd->lkhd", grad_scores, queries, preferred_element_type=F32)
        * score_scale
    )
    grad_qkv = (
        jnp.stack([grad_queries, grad_keys, grad_values]).astype(BF16).reshape(3, rows, width)
    )
    hidden_one_term = jnp.einsum("jrc,jkc->rk", grad_qkv, qkv_full, preferred_element_type=F32)
    qkv_grad = jnp.einsum("rk,jrc->jkc", full_one, grad_qkv, preferred_element_type=F32)
    bias_terms = jnp.concatenate(
        [
            jnp.sum(grad_qkv[0], 0, dtype=F32)[None],
            jnp.sum(grad_qkv[2], 0, dtype=F32)[None],
            proj_bias_grad,
            fc1_bias_grad.reshape(-1, width),
            fc2_bias_grad,
        ]
    )
    (
        tokens_grad, grad_mod_all, cond_terms, bias_sums, fc1_shard, proj_shard, qkv_shard
    ) = call(
        partial(tail_kernel, tok_count, scatter_orders),
        4,
        [
            own_f32, ((tok_count, 6, lat, width), F32), ((tok_count, every, part), F32),
            (bias_terms.shape, F32),
            ((part, inner), F32), ((part, width), F32), ((3, part, width), F32),
        ],
        scatter_bufs
        + [
            stats, ((lat * 2, width), F32), ((6, every, width), F32), ((FEAT, every, part), F32),
            ((tok_count - 1,) + bias_terms.shape, F32),
        ]
        + large_parts + small_parts
        + [((3, tok_count - 1, part, width), BF16)] * 2,
        (9, 7 * (tok_count - 1)),
        hidden_one_term.astype(BF16),
        normed_one,
        inverse_one,
        mod,
        grad_middle,
        two_sums,
        ada_weight,
        bias_terms,
        fc1_grad.astype(BF16).reshape(large),
        proj_grad.astype(BF16).reshape(small),
        qkv_grad.astype(BF16).reshape((3,) + small),
    )
    grad_mod_all = grad_mod_all.astype(BF16)
    ada_bias_sum = jnp.sum(grad_mod_all, (0, 2), dtype=F32)
    grad_mod_all = grad_mod_all.transpose(0, 2, 1, 3).reshape(every, 6, width)
    ada_shard = jnp.einsum("lk,ljc->jkc", cond_rows, grad_mod_all, preferred_element_type=F32)
    grad_cond_act = cond_terms.transpose(1, 0, 2).reshape(every, D)
    own_cond = lax.dynamic_index_in_dim(cond_all, feat_at, 1, False)[:, :width]
    own_grad = lax.dynamic_slice_in_dim(grad_cond_act, offset, width, 1)
    grad_condition = jax.vjp(jax.nn.silu, own_cond)[1](own_grad)[0]
    class_count = class_table.shape[1]
    one_hot = (
        labels_all[:, None] == jnp.arange(class_count, dtype=jnp.int32)[None, :]
    ).astype(F32)
    class_sum = jnp.einsum("lc,lw->wc", one_hot, grad_condition, precision=lax.Precision.HIGHEST)
    return (
        output.T,
        tokens_grad.T,
        class_sum,
        ada_shard,
        ada_bias_sum,
        qkv_shard,
        bias_sums[:2],
        proj_shard,
        bias_sums[2],
        fc1_shard,
        bias_sums[3:-1].reshape(-1),
        fc2_shard,
        bias_sums[-1],
    )


def solution(mesh):
    return jax.shard_map(
        partial(per_device, mesh.shape["tok"]),
        mesh=mesh,
        in_specs=(
            P("feat", "tok"),
            P("tok"),
            P("tok"),
            P("feat", None),
            P(None, "tok", "feat"),
            P(None, "feat"),
            P(None, "tok", "feat"),
            P(None, "feat"),
            P("tok", "feat"),
            P("feat"),
            P("tok", "feat"),
            P("feat"),
            P("tok", "feat"),
            P("feat"),
            P("feat", "tok"),
        ),
        out_specs=(
            P("feat", "tok"),
            P("feat", "tok"),
            P("feat", None),
            P(None, "tok", "feat"),
            P(None, "feat"),
            P(None, "tok", "feat"),
            P(None, "feat"),
            P("tok", "feat"),
            P("feat"),
            P("tok", "feat"),
            P("feat"),
            P("tok", "feat"),
            P("feat"),
        ),
        check_vma=False,
    )
```

```python
from functools import partial
import math

import jax
import jax.numpy as jnp
from jax import lax
from jax.experimental import pallas as pl
from jax.experimental.pallas import tpu as pltpu
from jax.sharding import PartitionSpec as P

D = 768
HEAD_DIM = 64
FEAT = 4
MESH = pl.DeviceIdType.MESH
F32 = jnp.float32
BF16 = jnp.bfloat16
VMEM = pl.BlockSpec(memory_space=pltpu.VMEM)


def time_features(step_ids, feat_count):
    half_width = feat_count // 2
    frequency = jnp.exp(-math.log(10000.0) * jnp.arange(half_width, dtype=jnp.float32) / half_width)
    angles = step_ids.astype(jnp.float32)[:, None] * frequency[None, :]
    return jnp.concatenate([jnp.cos(angles), jnp.sin(angles)], axis=-1)


def partners():
    f = lax.axis_index("feat")
    near = f + 1 - 2 * (f % 2)
    far = (f + 2) % FEAT
    return f, near, far, (near + 2) % FEAT


def greet(near, far, cross):
    barrier = pltpu.get_barrier_semaphore()
    for peer in (near, far, cross):
        pl.semaphore_signal(barrier, inc=1, device_id={"feat": peer}, device_id_type=MESH)
    pl.semaphore_wait(barrier, 3)


def push(src, dst, sems, at, peer):
    return pltpu.make_async_remote_copy(
        src_ref=src,
        dst_ref=dst,
        send_sem=sems.at[0, at],
        recv_sem=sems.at[1, at],
        device_id={"feat": peer},
        device_id_type=MESH,
    )


def gather_start(buf, sems, base):
    f, near, far, _ = partners()
    to_far = push(buf.at[f], buf.at[f], sems, base, far)
    to_near = push(buf.at[f], buf.at[f], sems, base + 1, near)
    to_far.start()
    to_near.start()
    return to_far, to_near


def gather_forward(buf, sems, base, started):
    _, near, far, _ = partners()
    started[0].wait_recv()
    relay = push(buf.at[far], buf.at[far], sems, base + 2, near)
    relay.start()
    return relay


def gather_finish(buf, out, started, relay):
    started[1].wait_recv()
    relay.wait_recv()
    for copy in (*started, relay):
        copy.wait_send()
    width = buf.shape[2]
    for block in range(FEAT):
        out[:, block * width : (block + 1) * width] = buf[block]


def scatter_start(term, buf, near_in, sems, base):
    f, near, _, _ = partners()
    side, core = f // 2, f % 2
    width = buf.shape[2]
    for block in range(FEAT):
        buf[block] = term[:, block * width : (block + 1) * width]
    first = push(buf.at[2 * (1 - side) + 1 - core], near_in.at[0], sems, base, near)
    second = push(buf.at[2 * side + 1 - core], near_in.at[1], sems, base + 1, near)
    first.start()
    second.start()
    return first, second


def scatter_cross(buf, near_in, out_buf, far_in, sems, base, started):
    _, _, far, _ = partners()
    started[0].wait_recv()
    out_buf[...] = (buf[far].astype(F32) + near_in[0].astype(F32)).astype(BF16)
    cross = push(out_buf, far_in, sems, base + 2, far)
    cross.start()
    return cross


def scatter_finish(buf, near_in, far_in, started, cross):
    f, _, _, _ = partners()
    started[1].wait_recv()
    own = buf[f].astype(F32) + near_in[1].astype(F32)
    cross.wait_recv()
    for copy in (*started, cross):
        copy.wait_send()
    return own + far_in[...].astype(F32)


def swap_rows(pair, stats, sems, base):
    _, near, far, cross = partners()
    rows = pair[0].shape[0]
    lane = lax.broadcasted_iota(jnp.int32, (rows, 128), 1)
    packed = jnp.where(lane == 0, pair[0], jnp.where(lane == 1, pair[1], 0.0))
    stats[0] = packed.T[:8]
    copies = [
        push(stats.at[0], stats.at[slot], sems, base + slot - 1, peer)
        for slot, peer in ((1, near), (2, far), (3, cross))
    ]
    for copy in copies:
        copy.start()
    for copy in copies:
        copy.wait()
    return stats[...]


def columns(first, second):
    rows = first.shape[1]
    tall = jnp.concatenate([first, second, jnp.zeros((126, rows), F32)], 0).T
    return tall[:, 0:1], tall[:, 1:2]


def norm_stats(values, stats, sems, base):
    width = values.shape[1]
    local = jnp.sum(values, 1, keepdims=True)
    off = values - local / width
    got = swap_rows((local, jnp.sum(off * off, 1, keepdims=True)), stats, sems, base)
    sums, squares = got[:, 0], got[:, 1]
    mean = jnp.sum(sums, 0, keepdims=True) / D
    shifted = sums / width - mean
    variance = jnp.sum(squares + width * shifted * shifted, 0, keepdims=True) / D
    return columns(mean, lax.rsqrt(variance + 1e-06))


def norm_grad(grad_norm, normed, inverse, stats, sems, base):
    got = swap_rows(
        (jnp.sum(grad_norm, 1, keepdims=True), jnp.sum(grad_norm * normed, 1, keepdims=True)),
        stats,
        sems,
        base,
    )
    total = jnp.sum(got, 0)
    first, second = columns(total[0:1] / D, total[1:2] / D)
    return inverse * (grad_norm - first - normed * second)


def spread(mod, which, rows):
    count = mod.shape[1]
    return jnp.concatenate(
        [
            jnp.broadcast_to(mod[which, l : l + 1], (rows // count, mod.shape[2]))
            for l in range(count)
        ],
        0,
    )


def latent_sums(out, values, which, kinds):
    count = out.shape[0] // kinds
    seq = values.shape[0] // count
    for l in range(count):
        row = l * kinds + which
        out[row : row + 1] = jnp.sum(values[l * seq : (l + 1) * seq], 0, keepdims=True)


def flip(t, *bits):
    for bit in bits:
        t = t + bit * (1 - 2 * ((t // bit) % 2))
    return t


def push_tok(src, dst, sems, at, peer):
    return pltpu.make_async_remote_copy(
        src_ref=src,
        dst_ref=dst,
        send_sem=sems.at[0, at],
        recv_sem=sems.at[1, at],
        device_id={"tok": peer},
        device_id_type=MESH,
    )


def greet_all(count):
    t = lax.axis_index("tok")
    _, near, far, cross = partners()
    barrier = pltpu.get_barrier_semaphore()
    for peer in (near, far, cross):
        pl.semaphore_signal(barrier, inc=1, device_id={"feat": peer}, device_id_type=MESH)
    for step in range(1, count):
        pl.semaphore_signal(
            barrier, inc=1, device_id={"tok": (t + step) % count}, device_id_type=MESH
        )
    pl.semaphore_wait(barrier, FEAT - 1 + count - 1)


def send_all(src, dst, sems, base, count):
    t = lax.axis_index("tok")
    copies = [
        push_tok(src, dst, sems, base + step - 1, (t + step) % count) for step in range(1, count)
    ]
    for copy in copies:
        copy.start()
    return copies


def wait_all(copies):
    for copy in copies:
        copy.wait()


def block_at(ref, block, lead, cols=None):
    if cols is not None:
        return ref.at[block, :, cols]
    return ref.at[:, block] if lead else ref.at[block]


def halves(ref):
    half = ref.shape[-1] // 2
    return pl.ds(0, half), pl.ds(half, half)


class RowGather:
    def __init__(self, block, full, lead, order, sems, base, cols=None):
        t = lax.axis_index("tok")
        self.full, self.lead, self.order, self.sems, self.base = full, lead, list(order), sems, base
        self.held, self.copies, self.cols = [()], [], cols
        block_at(full, t, lead, cols)[...] = block[...] if cols is None else block[:, cols]
        self.send()

    def send(self):
        t = lax.axis_index("tok")
        bit = self.order[0]
        self.copies = []
        for held in self.held:
            view = block_at(self.full, flip(t, *held), self.lead, self.cols)
            self.copies.append(push_tok(view, view, self.sems, self.base, flip(t, bit)))
            self.base += 1
        for copy in self.copies:
            copy.start()

    def step(self):
        if not self.order:
            return
        wait_all(self.copies)
        bit = self.order.pop(0)
        self.held = self.held + [held + (bit,) for held in self.held]
        if self.order:
            self.send()


class RowScatter:
    def __init__(self, grad, out, acc, recv, lead, order, sems, base, cols=None):
        self.out, self.acc, self.recv, self.lead = out, acc, recv, lead
        self.cols = cols
        self.order, self.sems, self.base = list(order), sems, base
        t = lax.axis_index("tok")
        self.own = lambda held: block_at(grad, flip(t, *held), lead, cols)
        self.slot = 0
        self.send()

    def send(self):
        t = lax.axis_index("tok")
        bit, rest = self.order[0], self.order[1:]
        self.kept = [()]
        for other in rest:
            self.kept = self.kept + [held + (other,) for held in self.kept]
        self.copies = [
            push_tok(
                self.own((bit,) + held),
                block_at(self.recv, self.slot + at, self.lead, self.cols),
                self.sems,
                self.base + self.slot + at,
                flip(t, bit),
            )
            for at, held in enumerate(self.kept)
        ]
        for copy in self.copies:
            copy.start()

    def step(self):
        if not self.order:
            return
        places = {}
        for at, held in enumerate(self.kept):
            self.copies[at].wait()
            slot = self.slot + at
            total = self.own(held)[...].astype(F32) + block_at(
                self.recv, slot, self.lead, self.cols
            )[...].astype(F32)
            if len(self.order) == 1 and self.cols is None:
                self.out[...] = total
            elif len(self.order) == 1:
                self.out[:, self.cols] = total
            else:
                block_at(self.acc, slot, self.lead, self.cols)[...] = total.astype(BF16)
            places[frozenset(held)] = slot
        self.slot += len(self.kept)
        self.order.pop(0)
        self.own = lambda held: block_at(
            self.acc, places[frozenset(held)], self.lead, self.cols
        )
        if self.order:
            self.send()


def head_kernel(
    count, orders,
    x, grad_out, cond, ada, bias, qkv, proj, fc1,
    full, grad_full, normed_out, inverse_out, fc2_sum, mod, cond_all, cond_act, qkv_full, proj_full, fc1_full,
    buf, grad_buf, stats, cond_rows, terms, got, sems, tok_sems,
):
    f, near, far, cross = partners()
    t = lax.axis_index("tok")
    rows, width = x.shape
    lat = cond.shape[0]
    part = ada.shape[1]
    greet_all(count)
    cond_all[t, f] = cond[...]
    shares = [
        push(cond_all.at[t, f], cond_all.at[t, f], sems, at, peer)
        for at, peer in enumerate((near, far, cross))
    ]
    for copy in shares:
        copy.start()
    each = count - 1
    weights = [RowGather(qkv, qkv_full, True, orders[0], tok_sems, 0)]
    wait_all(shares)
    sharing = send_all(cond_all.at[t], cond_all.at[t], tok_sems, 4 * each, count)
    weights.append(RowGather(proj, proj_full, False, orders[1], tok_sems, each))
    for at, cols in enumerate(halves(fc1)):
        weights.append(
            RowGather(fc1, fc1_full, False, orders[1 - at], tok_sems, (2 + at) * each, cols)
        )
    values = x[...]
    mean, inverse = norm_stats(values, stats, sems, 3)
    normed = (values - mean) * inverse
    normed_out[...] = normed
    inverse_out[...] = inverse
    wait_all(sharing)
    picked = jnp.zeros((count * lat, part), F32)
    for block in range(FEAT):
        for owner in range(count):
            cond_rows[block, owner * lat : (owner + 1) * lat] = cond_all[owner, block]
        value = cond_rows[block][:, :width]
        act = (value / (1.0 + jnp.exp(-value))).astype(BF16)
        chosen = (
            lax.broadcasted_iota(jnp.int32, (width, part), 0) + block * width
            == lax.broadcasted_iota(jnp.int32, (width, part), 1) + t * part
        )
        picked += jnp.dot(act, chosen.astype(F32).astype(BF16), preferred_element_type=F32)
    picked = picked.astype(BF16)
    cond_act[...] = picked
    for which in range(6):
        term = jnp.dot(picked, ada[which], preferred_element_type=F32)
        for owner in range(count):
            terms[owner, which] = term[owner * lat : (owner + 1) * lat]
    copies = [
        push_tok(terms.at[(t + step) % count], got.at[step - 1], tok_sems, 5 * each + step - 1, (t + step) % count)
        for step in range(1, count)
    ]
    for copy in copies:
        copy.start()
    wait_all(copies)
    mod[...] = terms[t] + jnp.sum(got[...], 0) + bias[...]
    mods = mod[...]
    buf[f] = (normed * (1.0 + spread(mods, 1, rows)) + spread(mods, 0, rows)).astype(BF16)
    started = gather_start(buf, sems, 6)
    for weight in weights:
        weight.step()
    grad_mlp = (grad_out[...] * spread(mods, 5, rows)).astype(BF16)
    fc2_sum[...] = jnp.sum(grad_mlp.astype(F32), 0, keepdims=True)
    grad_buf[f] = grad_mlp
    grad_started = gather_start(grad_buf, sems, 9)
    for weight in weights:
        weight.step()
    relay = gather_forward(buf, sems, 6, started)
    gather_finish(buf, full, started, relay)
    grad_relay = gather_forward(grad_buf, sems, 9, grad_started)
    gather_finish(grad_buf, grad_full, grad_started, grad_relay)
    for _ in range(count.bit_length()):
        for weight in weights:
            weight.step()


def middle_kernel(
    count, orders,
    term, x, mod, bias, fc2, fc2_full, attn_out, middle_out, normed_out, inverse_out, full,
    sbuf, near_in, out_buf, far_in, buf, stats, sems, tok_sems,
):
    f, near, far, cross = partners()
    rows = x.shape[0]
    mods = mod[...]
    greet_all(count)
    started = scatter_start(term, sbuf, near_in, sems, 0)
    weights = [
        RowGather(fc2, fc2_full, False, orders[1 - at], tok_sems, at * (count - 1), cols)
        for at, cols in enumerate(halves(fc2))
    ]
    crossing = scatter_cross(sbuf, near_in, out_buf, far_in, sems, 0, started)
    attn = scatter_finish(sbuf, near_in, far_in, started, crossing) + bias[...]
    attn_out[...] = attn
    for weight in weights:
        weight.step()
    middle = x[...] + spread(mods, 2, rows) * attn
    middle_out[...] = middle
    mean, inverse = norm_stats(middle, stats, sems, 3)
    normed = (middle - mean) * inverse
    normed_out[...] = normed
    inverse_out[...] = inverse
    buf[f] = (normed * (1.0 + spread(mods, 4, rows)) + spread(mods, 3, rows)).astype(BF16)
    gathering = gather_start(buf, sems, 6)
    for weight in weights:
        weight.step()
    relay = gather_forward(buf, sems, 6, gathering)
    gather_finish(buf, full, gathering, relay)
    for _ in range(count.bit_length()):
        for weight in weights:
            weight.step()


def back_kernel(
    count, orders,
    term, mlp_term, grad_out, normed_in, inverse_in, mod, bias, middle, attn, fc2,
    fc2_out, grad_middle_out, full, output, sums, proj_sum,
    sbuf, near_in, out_buf, far_in, mbuf, mnear, mout, mfar, buf, stats, fc2_acc, fc2_got, sems, tok_sems,
):
    f, near, far, cross = partners()
    rows = grad_out.shape[0]
    mods = mod[...]
    greet_all(count)
    started = scatter_start(term, sbuf, near_in, sems, 0)
    grads = [
        RowScatter(
            fc2, fc2_out, fc2_acc, fc2_got, False, orders[at], tok_sems, at * (count - 1), cols
        )
        for at, cols in enumerate(halves(fc2))
    ]
    mlp_started = scatter_start(mlp_term, mbuf, mnear, sems, 3)
    crossing = scatter_cross(sbuf, near_in, out_buf, far_in, sems, 0, started)
    grad_hidden = scatter_finish(sbuf, near_in, far_in, started, crossing)
    normed = normed_in[...]
    grad_middle = grad_out[...] + norm_grad(
        grad_hidden * (1.0 + spread(mods, 4, rows)), normed, inverse_in[...], stats, sems, 6
    )
    grad_attn = (grad_middle * spread(mods, 2, rows)).astype(BF16)
    buf[f] = grad_attn
    gathering = gather_start(buf, sems, 9)
    mlp_crossing = scatter_cross(mbuf, mnear, mout, mfar, sems, 3, mlp_started)
    for grad in grads:
        grad.step()
    grad_middle_out[...] = grad_middle
    proj_sum[...] = jnp.sum(grad_attn.astype(F32), 0, keepdims=True)
    latent_sums(sums, grad_hidden, 0, 4)
    latent_sums(sums, grad_hidden * normed, 1, 4)
    latent_sums(sums, grad_middle * attn[...], 2, 4)
    relay = gather_forward(buf, sems, 9, gathering)
    gather_finish(buf, full, gathering, relay)
    for grad in grads:
        grad.step()
    mlp_out = scatter_finish(mbuf, mnear, mfar, mlp_started, mlp_crossing) + bias[...]
    output[...] = middle[...] + spread(mods, 5, rows) * mlp_out
    latent_sums(sums, grad_out[...] * mlp_out, 3, 4)
    for _ in range(count.bit_length()):
        for grad in grads:
            grad.step()


def tail_kernel(
    count, orders,
    term, normed_in, inverse_in, mod, grad_middle, two_sums, ada, biases, fc1, proj, qkv,
    tokens_grad, grad_mod, cond_terms, bias_sums, fc1_out, proj_out, qkv_out,
    sbuf, near_in, out_buf, far_in, stats, ones, grad_rows, cond_parts, bias_got,
    fc1_acc, fc1_got, proj_acc, proj_got, qkv_acc, qkv_got, sems, tok_sems,
):
    _, near, far, cross = partners()
    t = lax.axis_index("tok")
    rows = normed_in.shape[0]
    mods = mod[...]
    lat = mods.shape[1]
    each = count - 1
    greet_all(count)
    started = scatter_start(term, sbuf, near_in, sems, 0)
    bias_copies = [
        push_tok(biases, bias_got.at[step - 1], tok_sems, 6 * each + step - 1, (t + step) % count)
        for step in range(1, count)
    ]
    for copy in bias_copies:
        copy.start()
    grads = [
        RowScatter(fc1, fc1_out, fc1_acc, fc1_got, False, orders[at], tok_sems, at * each, cols)
        for at, cols in enumerate(halves(fc1))
    ] + [
        RowScatter(proj, proj_out, proj_acc, proj_got, False, orders[1], tok_sems, 2 * each),
        RowScatter(qkv, qkv_out, qkv_acc, qkv_got, True, orders[0], tok_sems, 3 * each),
    ]
    crossing = scatter_cross(sbuf, near_in, out_buf, far_in, sems, 0, started)
    grad_hidden = scatter_finish(sbuf, near_in, far_in, started, crossing)
    normed = normed_in[...]
    latent_sums(ones, grad_hidden, 0, 2)
    latent_sums(ones, grad_hidden * normed, 1, 2)
    for l in range(lat):
        one, two = l * 2, l * 4
        kept = (
            ones[one : one + 1],
            ones[one + 1 : one + 2],
            two_sums[two + 2 : two + 3],
            two_sums[two : two + 1],
            two_sums[two + 1 : two + 2],
            two_sums[two + 3 : two + 4],
        )
        for which in range(6):
            grad_mod[t, which, l : l + 1] = kept[which]
    mod_copies = send_all(grad_mod.at[t], grad_mod.at[t], tok_sems, 4 * each, count)
    tokens_grad[...] = grad_middle[...] + norm_grad(
        grad_hidden * (1.0 + spread(mods, 1, rows)), normed, inverse_in[...], stats, sems, 3
    )
    for grad in grads[:2]:
        grad.step()
    wait_all(mod_copies)
    total = None
    for which in range(6):
        for owner in range(count):
            grad_rows[which, owner * lat : (owner + 1) * lat] = grad_mod[owner, which]
        piece = lax.dot_general(
            grad_rows[which].astype(BF16), ada[which], (((1,), (1,)), ((), ())),
            preferred_element_type=F32,
        )
        total = piece if total is None else total + piece
    cond_parts[0] = total
    copies = [
        push(cond_parts.at[0], cond_parts.at[slot], sems, 5 + slot, peer)
        for slot, peer in ((1, near), (2, far), (3, cross))
    ]
    for copy in copies:
        copy.start()
    for grad in grads[2:]:
        grad.step()
    wait_all(copies)
    cond_terms[t] = (cond_parts[0] + cond_parts[1]) + (cond_parts[2] + cond_parts[3])
    cond_copies = send_all(cond_terms.at[t], cond_terms.at[t], tok_sems, 5 * each, count)
    for _ in range(count.bit_length()):
        for grad in grads:
            grad.step()
    wait_all(bias_copies)
    bias_sums[...] = biases[...] + jnp.sum(bias_got[...], 0)
    wait_all(cond_copies)


def call(kernel, collective_id, outs, scratch, sem_counts, *args):
    out_shape = [jax.ShapeDtypeStruct(shape, dtype) for shape, dtype in outs]
    return pl.pallas_call(
        kernel,
        out_shape=out_shape,
        in_specs=[VMEM] * len(args),
        out_specs=[VMEM] * len(outs),
        scratch_shapes=[pltpu.VMEM(shape, dtype) for shape, dtype in scratch]
        + [pltpu.SemaphoreType.DMA((2, count)) for count in sem_counts],
        compiler_params=pltpu.CompilerParams(
            collective_id=collective_id, has_side_effects=True, vmem_limit_bytes=40 * 2**20
        ),
    )(*args)


def per_device(
    tok_count,
    tokens,
    timesteps,
    labels,
    class_table,
    ada_weight,
    ada_bias,
    qkv_weight,
    qv_bias,
    proj_weight,
    proj_bias,
    fc1_weight,
    fc1_bias,
    fc2_weight,
    fc2_bias,
    cotangent,
):
    width, rows = tokens.shape
    lat = timesteps.shape[0]
    seq_len = rows // lat
    head_count = width // HEAD_DIM
    score_scale = HEAD_DIM ** (-0.5)
    feat_at = lax.axis_index("feat")
    offset = feat_at * width
    head_shape = (lat, seq_len, head_count, HEAD_DIM)
    part = ada_weight.shape[1]
    bits = [tok_count >> (i + 1) for i in range(tok_count.bit_length() - 1)]
    gather_orders = (bits, bits[-1:] + bits[:-1])
    scatter_orders = tuple(order[::-1] for order in gather_orders)
    lanes = -(-(width + 1) // 128) * 128
    every = tok_count * lat

    waves = lax.dynamic_slice_in_dim(time_features(timesteps, D), offset, width, 1)
    condition = jnp.take(class_table, labels, axis=1).T.astype(F32) + waves
    own_f32 = ((rows, width), F32)
    own_low = ((rows, width), BF16)
    one_f32 = ((rows, 1), F32)
    full_low = ((rows, D), BF16)
    line = ((1, width), F32)
    buf = ((FEAT, rows, width), BF16)
    stats = ((FEAT, 8, rows), F32)
    scatter_bufs = [buf, ((2, rows, width), BF16), own_low, own_low]

    cond_sent = jnp.concatenate(
        [condition, labels.astype(F32)[:, None], jnp.zeros((lat, lanes - width - 1), F32)], 1
    )
    mod_shape = ((6, lat, width), F32)
    inner = fc1_bias.shape[0]
    small = (tok_count, part, width)
    large = (tok_count, part, inner)
    small_parts = [((tok_count - 1, part, width), BF16)] * 2
    large_parts = [((tok_count - 1, part, inner), BF16)] * 2
    field_in = tokens.T
    grad_out = cotangent.T
    (
        full_one, grad_mlp_full, normed_one, inverse_one, fc2_bias_grad, mod, cond_all, cond_rows,
        qkv_full, proj_full, fc1_full,
    ) = call(
        partial(head_kernel, tok_count, gather_orders),
        0,
        [
            full_low, full_low, own_f32, one_f32, line, mod_shape,
            ((tok_count, FEAT, lat, lanes), F32), ((every, part), BF16),
            ((3,) + small, BF16), (small, BF16), (large, BF16),
        ],
        [
            buf, buf, stats, ((FEAT, every, lanes), F32),
            ((tok_count, 6, lat, width), F32), ((tok_count - 1, 6, lat, width), F32),
        ],
        (12, 6 * (tok_count - 1)),
        field_in,
        grad_out,
        cond_sent,
        ada_weight,
        ada_bias[:, None],
        qkv_weight,
        proj_weight,
        fc1_weight,
    )
    qkv_full = qkv_full.reshape(3, D, width)
    proj_full = proj_full.reshape(D, width)
    fc1_full = fc1_full.reshape(D, inner)
    cond_all = cond_all.transpose(0, 2, 1, 3).reshape(every, FEAT, lanes)
    labels_all = cond_all[:, 0, width].astype(jnp.int32)
    projected = jnp.einsum("rk,jkc->jrc", full_one, qkv_full, preferred_element_type=F32)
    queries = (projected[0] + qv_bias[0]).astype(BF16).reshape(head_shape)
    keys_low = projected[1].astype(BF16).reshape(head_shape)
    values_low = (projected[2] + qv_bias[1]).astype(BF16).reshape(head_shape)
    scores = (
        jnp.einsum("lqhd,lkhd->lhqk", queries, keys_low, preferred_element_type=F32) * score_scale
    )
    top_score = jnp.max(scores, -1, keepdims=True)
    exponent = jnp.exp(scores - top_score)
    exp_sums = jnp.sum(exponent, -1, keepdims=True)
    probs = exponent / exp_sums
    probs_low = probs.astype(BF16)
    attended = jnp.einsum("lhqk,lkhd->lqhd", probs_low, values_low, preferred_element_type=F32)
    attended = attended.astype(BF16).reshape(rows, width)
    attn_term = jnp.einsum("rc,oc->ro", attended, proj_full, preferred_element_type=F32)
    fc2_full, attn_out, middle, normed_two, inverse_two, full_two = call(
        partial(middle_kernel, tok_count, gather_orders),
        2,
        [(large, BF16), own_f32, own_f32, own_f32, one_f32, full_low],
        scatter_bufs + [buf, stats],
        (9, 2 * (tok_count - 1)),
        attn_term.astype(BF16),
        field_in,
        mod,
        proj_bias[None],
        fc2_weight,
    )
    fc2_full = fc2_full.reshape(D, inner)
    pre_act = jnp.dot(full_two, fc1_full, preferred_element_type=F32) + fc1_bias
    act_value, gelu_back = jax.vjp(partial(jax.nn.gelu, approximate=True), pre_act)
    act_low = act_value.astype(BF16)
    grad_act = jnp.dot(grad_mlp_full, fc2_full, preferred_element_type=F32)
    grad_pre = gelu_back(grad_act)[0].astype(BF16)
    mlp_term = jnp.einsum("rf,of->ro", act_low, fc2_full, preferred_element_type=F32)
    hidden_two_term = jnp.einsum("rf,kf->rk", grad_pre, fc1_full, preferred_element_type=F32)
    fc2_grad = jnp.einsum("ro,rf->of", grad_mlp_full, act_low, preferred_element_type=F32)
    fc2_shard, grad_middle, grad_attn_full, output, two_sums, proj_bias_grad = call(
        partial(back_kernel, tok_count, scatter_orders),
        3,
        [((part, inner), F32), own_f32, full_low, own_f32, ((lat * 4, width), F32), line],
        scatter_bufs + scatter_bufs + [buf, stats] + large_parts,
        (12, 2 * (tok_count - 1)),
        hidden_two_term.astype(BF16),
        mlp_term.astype(BF16),
        grad_out,
        normed_two,
        inverse_two,
        mod,
        fc2_bias[None],
        middle,
        attn_out,
        fc2_grad.astype(BF16).reshape(large),
    )
    fc1_bias_grad = jnp.sum(grad_pre, 0, dtype=F32)
    fc1_grad = jnp.einsum("rk,rf->kf", full_two, grad_pre, preferred_element_type=F32)
    proj_grad = jnp.einsum("ro,rc->oc", grad_attn_full, attended, preferred_element_type=F32)
    grad_attended = (
        jnp.dot(grad_attn_full, proj_full, preferred_element_type=F32)
        .astype(BF16)
        .reshape(head_shape)
    )
    grad_values = jnp.einsum(
        "lhqk,lqhd->lkhd", probs_low, grad_attended, preferred_element_type=F32
    )
    grad_probs = jnp.einsum(
        "lqhd,lkhd->lhqk", grad_attended, values_low, preferred_element_type=F32
    )
    grad_scores = (
        probs * (grad_probs - jnp.sum(grad_probs * probs, -1, keepdims=True))
    ).astype(BF16)
    grad_queries = (
        jnp.einsum("lhqk,lkhd->lqhd", grad_scores, keys_low, preferred_element_type=F32)
        * score_scale
    )
    grad_keys = (
        jnp.einsum("lhqk,lqhd->lkhd", grad_scores, queries, preferred_element_type=F32)
        * score_scale
    )
    grad_qkv = (
        jnp.stack([grad_queries, grad_keys, grad_values]).astype(BF16).reshape(3, rows, width)
    )
    hidden_one_term = jnp.einsum("jrc,jkc->rk", grad_qkv, qkv_full, preferred_element_type=F32)
    qkv_grad = jnp.einsum("rk,jrc->jkc", full_one, grad_qkv, preferred_element_type=F32)
    bias_terms = jnp.concatenate(
        [
            jnp.sum(grad_qkv[0], 0, dtype=F32)[None],
            jnp.sum(grad_qkv[2], 0, dtype=F32)[None],
            proj_bias_grad,
            fc1_bias_grad.reshape(-1, width),
            fc2_bias_grad,
        ]
    )
    (
        tokens_grad, grad_mod_all, cond_terms, bias_sums, fc1_shard, proj_shard, qkv_shard
    ) = call(
        partial(tail_kernel, tok_count, scatter_orders),
        4,
        [
            own_f32, ((tok_count, 6, lat, width), F32), ((tok_count, every, part), F32),
            (bias_terms.shape, F32),
            ((part, inner), F32), ((part, width), F32), ((3, part, width), F32),
        ],
        scatter_bufs
        + [
            stats, ((lat * 2, width), F32), ((6, every, width), F32), ((FEAT, every, part), F32),
            ((tok_count - 1,) + bias_terms.shape, F32),
        ]
        + large_parts + small_parts
        + [((3, tok_count - 1, part, width), BF16)] * 2,
        (9, 7 * (tok_count - 1)),
        hidden_one_term.astype(BF16),
        normed_one,
        inverse_one,
        mod,
        grad_middle,
        two_sums,
        ada_weight,
        bias_terms,
        fc1_grad.astype(BF16).reshape(large),
        proj_grad.astype(BF16).reshape(small),
        qkv_grad.astype(BF16).reshape((3,) + small),
    )
    grad_mod_all = grad_mod_all.astype(BF16)
    ada_bias_sum = jnp.sum(grad_mod_all, (0, 2), dtype=F32)
    grad_mod_all = grad_mod_all.transpose(0, 2, 1, 3).reshape(every, 6, width)
    ada_shard = jnp.einsum("lk,ljc->jkc", cond_rows, grad_mod_all, preferred_element_type=F32)
    grad_cond_act = cond_terms.transpose(1, 0, 2).reshape(every, D)
    own_cond = lax.dynamic_index_in_dim(cond_all, feat_at, 1, False)[:, :width]
    own_grad = lax.dynamic_slice_in_dim(grad_cond_act, offset, width, 1)
    grad_condition = jax.vjp(jax.nn.silu, own_cond)[1](own_grad)[0]
    class_count = class_table.shape[1]
    one_hot = (
        labels_all[:, None] == jnp.arange(class_count, dtype=jnp.int32)[None, :]
    ).astype(F32)
    class_sum = jnp.einsum("lc,lw->wc", one_hot, grad_condition, precision=lax.Precision.HIGHEST)
    return (
        output.T,
        tokens_grad.T,
        class_sum,
        ada_shard,
        ada_bias_sum,
        qkv_shard,
        bias_sums[:2],
        proj_shard,
        bias_sums[2],
        fc1_shard,
        bias_sums[3:-1].reshape(-1),
        fc2_shard,
        bias_sums[-1],
    )


def solution(mesh):
    return jax.shard_map(
        partial(per_device, mesh.shape["tok"]),
        mesh=mesh,
        in_specs=(
            P("feat", "tok"),
            P("tok"),
            P("tok"),
            P("feat", None),
            P(None, "tok", "feat"),
            P(None, "feat"),
            P(None, "tok", "feat"),
            P(None, "feat"),
            P("tok", "feat"),
            P("feat"),
            P("tok", "feat"),
            P("feat"),
            P("tok", "feat"),
            P("feat"),
            P("feat", "tok"),
        ),
        out_specs=(
            P("feat", "tok"),
            P("feat", "tok"),
            P("feat", None),
            P(None, "tok", "feat"),
            P(None, "feat"),
            P(None, "tok", "feat"),
            P(None, "feat"),
            P("tok", "feat"),
            P("feat"),
            P("tok", "feat"),
            P("feat"),
            P("tok", "feat"),
            P("feat"),
        ),
        check_vma=False,
    )
```
